256 devices in a mesh: fsdp: 64 (over x, y, z_hi), ctx: 4 (over z_lo, core).
Axes of the slice: x: 4, y: 4, z: 8 (z_hi: 4, z_lo: 2; z = z_hi * 2 + z_lo), core: 2. Of those that a mesh axis runs over, the one named last changes fastest.
Arguments:
- hidden_input: bfloat16 [64, 1024, 4096], P('fsdp', 'ctx'), may hold values from -22 to 22
- input_norm_gain: bfloat16 [4096], replicated, may hold values from 0.25 to 1.75
- packed_weight_codes: int32 [64, 16, 3072], P('fsdp'), may hold values from 0 to 65535
- group_scale_zeros: bfloat16 [64, 2, 3072], P('fsdp'), may hold values from 0 to 10, as said below
- adapter_down_weight: bfloat16 [4096, 128], replicated, may hold values from -0.09375 to 0.09375
- query_up_weight: bfloat16 [64, 2048], replicated, may hold values from -0.75 to 0.75
- value_up_weight: bfloat16 [64, 512], replicated, may hold values from -0.75 to 0.75
- document_index: int32 [64, 1024], P('fsdp'), may hold values from 0 to 5, never falling along the last dimension, each value on 1 to 512 neighbouring positions
- cotangent: bfloat16 [64, 1024, 2048], P('fsdp', 'ctx'), may hold values from -0.119628906 to 0.119628906
Outputs:
- context: bfloat16 [64, 1024, 2048], P('fsdp', 'ctx')
- grad_down: float32 [4096, 128], P(('fsdp', 'ctx'))
- query_up_gradient: float32 [64, 2048], replicated
- value_up_gradient: float32 [64, 512], replicated
The draws below stay inside these ranges and needn't reach their ends.
Inputs may be any that keep to these rules, and one draw needn't show every extreme that they name: `document_index`: along each sequence, in position order, document numbers never fall; every number from 0 appears, each document covers 1 to 512 positions and one covers exactly 512. `group_scale_zeros`: entry 0 of the second dimension is a positive scale, entry 1 a zero point of at least 5. `packed_weight_codes`: the int32 words may travel between devices as given, four codes a word; every other value crosses in 16 bits or more.
All inputs are finite; a program needn't handle non-finite values.
Results may differ from the reference program's by a relative error of at most 0.015.
The reference program's roundings to bfloat16 on the way count: a program that leaves them out, or rounds other values in their place, can miss the bound.
Values may be sent and summed in bfloat16 or wider, within the bound.
No kernel may reach another device: no remote copies, remote signals or barrier semaphores. Data moves between devices by JAX's collectives and lax.ppermute only.
A program may use at most 128 MiB of HBM per device.

```python
import math
import jax
import jax.numpy as jnp
import numpy as np
from jax import lax

MODEL_WIDTH = 4096
QUERY_HEADS = 16
KEY_VALUE_HEADS = 4
HEAD_WIDTH = 128
ADAPTER_RANK = 64
GROUP = 64
SEQ_LEN = 1024
DOCS = 6
SEQS = 64
QKV = 3072
N_CTX = 4


def draw_hidden_input(key, part):
    key = jax.random.fold_in(key, 17)
    first_key = jax.random.fold_in(key, 0)
    third_key = jax.random.fold_in(key, 2)
    base_values = jnp.clip(jax.random.normal(first_key, (SEQS, SEQ_LEN, MODEL_WIDTH), jnp.float32), -4.0, 4.0)
    column_scale = jnp.exp(jax.random.uniform(third_key, (MODEL_WIDTH,), jnp.float32, math.log(0.3), math.log(3.0)))
    values = base_values * column_scale
    return values.astype(jnp.bfloat16)


def draw_group_scale_zeros(key, part):
    key = jax.random.fold_in(key, 29)
    first_key, second_key = jax.random.split(key, 2)
    scales = jnp.exp(jax.random.uniform(first_key, (MODEL_WIDTH // GROUP, 1, QKV), jnp.float32, math.log(0.5), math.log(2.0))) * (0.2 / math.sqrt(MODEL_WIDTH))
    zeros_at = jax.random.uniform(second_key, (MODEL_WIDTH // GROUP, 1, QKV), jnp.float32, 5.0, 10.0)
    return jnp.concatenate([scales, zeros_at], axis=1).astype(jnp.bfloat16)


def plant(result, rng, least, largest):
    spot = [jax.random.randint(jax.random.fold_in(rng, axis), (), 0, length) for axis, length in enumerate(result.shape)]
    widest = result.shape.index(max(result.shape))
    next_to = spot[:widest] + [(spot[widest] + 1) % result.shape[widest]] + spot[widest + 1:]
    return result.at[tuple(spot)].set(least).at[tuple(next_to)].set(largest)


def shard_levels(stream_key, dims, shards, low, top_value):
    loudness, own = 1.0, jax.random.fold_in(stream_key, 6)
    for position, shards_of in shards:
        heights = jnp.exp(jax.random.uniform(jax.random.fold_in(own, position), (shards_of,), jnp.float32, low / len(shards), top_value / len(shards)))
        loudness = loudness * jnp.repeat(heights, dims[position] // shards_of).reshape([-1 if axis == position else 1 for axis in range(len(dims))])
    return loudness


def profile(amount, total, reach, slope):
    loads = [(1 << 20) // math.isqrt(standing ** slope) + 1 for standing in range(2, amount + 1)]
    rest, given = total - reach - (amount - 1), [1] * (amount - 1)
    while rest > 0:
        candidates = [i for i in range(amount - 1) if given[i] < reach]
        pool, budget = sum([loads[i] for i in candidates]), rest
        for i in candidates:
            more = min(reach - given[i], max(1, budget * loads[i] // pool), rest)
            given[i] = given[i] + more
            rest = rest - more
    return np.array([reach] + given)


def uneven_parts(stream_key, number_of, total, bound, slope):
    if number_of == 2:
        one = jax.random.randint(stream_key, (), max(1, total - bound), min(bound, total - 1) + 1)
        return jnp.stack([one, total - one])
    sizes = jnp.asarray(profile(number_of, total, bound, slope), jnp.int32)
    twos = (number_of - 1) // 2
    donor, receiver = sizes[1:1 + 2 * twos:2], sizes[2:2 + 2 * twos:2]
    slack = jnp.minimum(donor - 1, bound - receiver)
    moved = jax.random.randint(jax.random.fold_in(stream_key, 1), (twos,), 0, 1 << 20) % (slack + 1)
    sizes = sizes.at[1:1 + 2 * twos:2].set(donor - moved).at[2:2 + 2 * twos:2].set(receiver + moved)
    return sizes[jax.random.permutation(jax.random.fold_in(stream_key, 2), number_of)]


def centred(stream_key, dims, spread, reach, cuts=(), held_as=jnp.bfloat16):
    array = jax.random.normal(stream_key, dims, jnp.float32) * spread
    if len(cuts) > 0:
        array = shard_levels(stream_key, dims, cuts, -0.22, 0.18) * array
    return jnp.clip(array, min=-reach, max=reach).astype(held_as)


def setup_inputs(seed: int = 0) -> dict:
    streams_of = jax.random.split(jax.random.key(seed), 10)
    return {
        "hidden_input": draw_hidden_input(jax.random.fold_in(streams_of[9], 71), 0),
        "input_norm_gain": jnp.clip(1.0 + 0.15 * jax.random.normal(streams_of[1], (MODEL_WIDTH,), jnp.float32), 0.25, 1.75).astype(jnp.bfloat16),
        "packed_weight_codes": plant(jax.random.randint(streams_of[2], (MODEL_WIDTH // GROUP, GROUP // 4, QKV), 0, 65536), jax.random.fold_in(streams_of[2], 1), 0, 65535).astype(jnp.int32),
        "group_scale_zeros": draw_group_scale_zeros(jax.random.fold_in(streams_of[9], 71), 0),
        "adapter_down_weight": centred(streams_of[4], (MODEL_WIDTH, 2 * ADAPTER_RANK), MODEL_WIDTH ** -0.5, 0.09375),
        "query_up_weight": centred(streams_of[5], (ADAPTER_RANK, QUERY_HEADS * HEAD_WIDTH), ADAPTER_RANK ** -0.5, 0.75),
        "value_up_weight": centred(streams_of[6], (ADAPTER_RANK, KEY_VALUE_HEADS * HEAD_WIDTH), ADAPTER_RANK ** -0.5, 0.75),
        "document_index": jax.vmap(lambda own: jnp.searchsorted(jnp.cumsum(uneven_parts(own, DOCS, SEQ_LEN, SEQ_LEN // 2, 2)), jnp.arange(SEQ_LEN), side="right"))(jax.random.split(streams_of[7], SEQS)).reshape((SEQS, SEQ_LEN)).astype(jnp.int32),
        "cotangent": centred(streams_of[8], (SEQS, SEQ_LEN, QUERY_HEADS * HEAD_WIDTH), 0.02, 0.119628906, ((0, 64), (1, 4))),
    }


adapter_scale = 0.25
norm_eps = 1e-05
rope_theta = 500000.0

def frequencies(head_size):
    exponent = jnp.arange(0, head_size, 2, dtype=jnp.float32) / head_size
    inverse = 1.0 / rope_theta ** exponent
    wavelength = 2.0 * math.pi / inverse
    blend = (8192.0 / wavelength - 1.0) / 3.0
    middle = (1.0 - blend) * inverse / 8.0 + blend * inverse
    return jnp.where(wavelength < 2048.0, inverse, jnp.where(wavelength > 8192.0, inverse / 8.0, middle))

def storage_positions(storage, block_len, parts):
    owner = storage // (2 * block_len)
    second = storage // block_len % 2
    piece = jnp.where(second == 0, owner, 2 * parts - 1 - owner)
    return (piece * block_len + storage % block_len).astype(jnp.int32)

def rotate(values, positions, sign):
    half_size = values.shape[-1] // 2
    angles = positions.astype(jnp.float32)[:, None] * frequencies(values.shape[-1])[None, :]
    cosine = jnp.cos(angles)[:, None, :]
    sine = sign * jnp.sin(angles)[:, None, :]
    first_half = values[..., :half_size]
    second_half = values[..., half_size:]
    return jnp.concatenate([first_half * cosine - second_half * sine, second_half * cosine + first_half * sine], axis=-1)

def rms_norm(rows_in, gain):
    wide = rows_in.astype(jnp.float32)
    mean_square = lax.optimization_barrier(jnp.mean(wide * wide, axis=-1, keepdims=True))
    return (wide * lax.rsqrt(mean_square + norm_eps) * gain.astype(jnp.float32)).astype(jnp.bfloat16)

def dequantize(packed, qparams):
    shifts = 4 * jnp.arange(4, dtype=jnp.int32)
    nibbles = jnp.bitwise_and(jnp.right_shift(packed[:, :, None, :], shifts[None, None, :, None]), 15)
    group_count, word_count, _, column_count = nibbles.shape
    codes_wide = nibbles.reshape(group_count, word_count * 4, column_count).astype(jnp.float32)
    scales = qparams[:, 0:1, :].astype(jnp.float32)
    zeros_at = qparams[:, 1:2, :].astype(jnp.float32)
    return ((codes_wide - zeros_at) * scales).reshape(group_count * word_count * 4, column_count).astype(jnp.bfloat16)

def attend(queries, key_rows, value_row_block, upstream, query_docs, key_docs, query_pos, key_pos):
    count = queries.shape[0]
    grouped = queries.reshape(count, KEY_VALUE_HEADS, -1, HEAD_WIDTH).astype(jnp.float32)
    grad_out = upstream.reshape(count, KEY_VALUE_HEADS, -1, HEAD_WIDTH).astype(jnp.float32)
    key_wide = key_rows.astype(jnp.float32)
    value_wide = value_row_block.astype(jnp.float32)
    inverse_root = 1.0 / math.sqrt(HEAD_WIDTH)
    scores = jnp.einsum('qhgd,khd->hgqk', grouped, key_wide) * inverse_root
    allowed = (query_docs[:, None] == key_docs[None, :]) & (key_pos[None, :] <= query_pos[:, None])
    scores = jnp.where(allowed, scores, -1e+30)
    attention = jax.nn.softmax(scores, axis=-1)
    attention_low = attention.astype(jnp.bfloat16)
    low_wide = attention_low.astype(jnp.float32)
    context = jnp.einsum('hgqk,khd->qhgd', low_wide, value_wide).astype(jnp.bfloat16).reshape(count, -1)
    grad_attention = jnp.einsum('qhgd,khd->hgqk', grad_out, value_wide)
    row_dot = lax.optimization_barrier(jnp.sum(attention * grad_attention, axis=-1, keepdims=True))
    grad_scores = (attention * (grad_attention - row_dot) * inverse_root).astype(jnp.bfloat16)
    grad_query = jnp.einsum('hgqk,khd->qhgd', grad_scores.astype(jnp.float32), key_wide).reshape(count, -1, HEAD_WIDTH)
    grad_value = jnp.einsum('hgqk,qhgd->khd', low_wide, grad_out)
    return (context, grad_query, grad_value)

def reference(hidden_input, input_norm_gain, packed_weight_codes, group_scale_zeros, adapter_down_weight, query_up_weight, value_up_weight, document_index, cotangent):
    seq_count, seq_len, width = hidden_input.shape
    adapter_rank_size = query_up_weight.shape[0]
    query_width = query_up_weight.shape[1]
    key_value_width = value_up_weight.shape[1]
    normed_input = rms_norm(hidden_input.reshape(seq_count * seq_len, width), input_norm_gain)
    weights = dequantize(packed_weight_codes, group_scale_zeros)
    base_output = jnp.dot(normed_input, weights, preferred_element_type=jnp.float32).astype(jnp.bfloat16)
    adapter_input = jnp.dot(normed_input, adapter_down_weight, preferred_element_type=jnp.float32).astype(jnp.bfloat16)
    storage = jnp.arange(seq_len, dtype=jnp.int32)
    positions = storage_positions(storage, seq_len // (2 * N_CTX), N_CTX)
    row_positions = jnp.tile(positions, seq_count)
    query_before_adapter = base_output[:, :query_width].astype(jnp.float32) + adapter_scale * jnp.dot(adapter_input[:, :adapter_rank_size], query_up_weight, preferred_element_type=jnp.float32)
    queries = rotate(query_before_adapter.reshape(-1, QUERY_HEADS, HEAD_WIDTH), row_positions, 1.0).astype(jnp.bfloat16)
    key_pre = base_output[:, query_width:query_width + key_value_width].astype(jnp.float32)
    key_rows = rotate(key_pre.reshape(-1, KEY_VALUE_HEADS, HEAD_WIDTH), row_positions, 1.0).astype(jnp.bfloat16)
    value_row_block = (base_output[:, query_width + key_value_width:].astype(jnp.float32) + adapter_scale * jnp.dot(adapter_input[:, adapter_rank_size:], value_up_weight, preferred_element_type=jnp.float32)).astype(jnp.bfloat16)
    documents = jnp.take(document_index, positions, axis=1)

    def one_sequence(inputs):
        query_seq, key_seq, value_seq, grad_seq, doc_seq = inputs
        return attend(query_seq, key_seq, value_seq, grad_seq, doc_seq, doc_seq, positions, positions)
    context, grad_query, grad_value = lax.map(one_sequence, (queries.reshape(seq_count, seq_len, QUERY_HEADS, HEAD_WIDTH), key_rows.reshape(seq_count, seq_len, KEY_VALUE_HEADS, HEAD_WIDTH), value_row_block.reshape(seq_count, seq_len, KEY_VALUE_HEADS, HEAD_WIDTH), cotangent, documents))
    query_gradient = rotate(grad_query.reshape(-1, QUERY_HEADS, HEAD_WIDTH), row_positions, -1.0).reshape(-1, query_width).astype(jnp.bfloat16)
    value_gradient = grad_value.reshape(-1, key_value_width).astype(jnp.bfloat16)
    contract_axes = (((0,), (0,)), ((), ()))
    across_axes = (((1,), (1,)), ((), ()))
    query_up_gradient = adapter_scale * lax.dot_general(adapter_input[:, :adapter_rank_size], query_gradient, contract_axes, preferred_element_type=jnp.float32)
    value_up_gradient = adapter_scale * lax.dot_general(adapter_input[:, adapter_rank_size:], value_gradient, contract_axes, preferred_element_type=jnp.float32)
    adapter_gradient = jnp.concatenate([adapter_scale * lax.dot_general(query_gradient, query_up_weight, across_axes, preferred_element_type=jnp.float32), adapter_scale * lax.dot_general(value_gradient, value_up_weight, across_axes, preferred_element_type=jnp.float32)], axis=1).astype(jnp.bfloat16)
    grad_down = lax.dot_general(normed_input, adapter_gradient, contract_axes, preferred_element_type=jnp.float32)
    return (context, grad_down, query_up_gradient, value_up_gradient)
```

```python
import functools
import math

import jax
import jax.numpy as jnp
import numpy as np
from jax import lax
from jax.experimental import pallas as pl
from jax.experimental.pallas import tpu as pltpu
from jax.sharding import PartitionSpec as P

HEAD = 128
SCALE = 0.25
EPS = 1e-05
THETA = 500000.0
ROOT = 1.0 / math.sqrt(HEAD)
AXES = ("fsdp", "ctx")
VMEM = 60 * 1024 * 1024
F32, BF16, I32 = jnp.float32, jnp.bfloat16, jnp.int32


def place(l):
    f, c = divmod(l, 4)
    return [f // 16, f // 4 % 4, f % 4, c // 2, c % 2]


def index(p):
    return ((p[0] * 4 + p[1]) * 4 + p[2]) * 4 + p[3] * 2 + p[4]


SIZES = (4, 4, 4, 2, 2)
X, Y, Z, PAIR, CORE = range(5)


def take_from(value, axis, step):
    pairs = []
    for l in range(256):
        p = place(l)
        p[axis] = (p[axis] - step) % SIZES[axis]
        pairs.append((l, index(p)))
    return lax.ppermute(value, AXES, pairs)


def gather_axis(value, axis):
    return [value] + [take_from(value, axis, r) for r in (1, 2, 3)]


def absolute(parts, coordinate):
    twice = jnp.stack(parts + parts)
    return lax.dynamic_slice_in_dim(twice, (4 - coordinate) % 4, 4, 0)


def scatter_axis(pieces, axis, coordinate, narrow=False):
    own = lax.dynamic_index_in_dim(pieces, coordinate, 0, keepdims=False)
    sent = pieces.astype(BF16) if narrow else pieces
    got = [
        take_from(
            lax.dynamic_index_in_dim(sent, (coordinate + 4 - r) % 4, 0, keepdims=False), axis, r
        )
        for r in (1, 2, 3)
    ]
    return own + got[0].astype(F32) + got[1].astype(F32) + got[2].astype(F32)


def frequencies():
    exponent = jnp.arange(0, HEAD, 2, dtype=F32) / HEAD
    inverse = 1.0 / THETA**exponent
    wavelength = 2.0 * math.pi / inverse
    blend = (8192.0 / wavelength - 1.0) / 3.0
    middle = (1.0 - blend) * inverse / 8.0 + blend * inverse
    return jnp.where(
        wavelength < 2048.0, inverse, jnp.where(wavelength > 8192.0, inverse / 8.0, middle)
    )


def scale_code(scale):
    m = scale.astype(F32) * 16.0
    e = jnp.full(m.shape, 4, I32)
    for k in (64, 64, 32, 16, 8, 4, 2, 1):
        small = m < 2.0 ** (8 - k)
        m = jnp.where(small, m * 2.0**k, m)
        e = jnp.where(small, e + k, e)
    return m.astype(I32) + 256 * e


def decode_scale(code):
    s = jnp.bitwise_and(code, 255).astype(F32)
    e = jnp.right_shift(code, 8)
    for k in (1, 2, 4, 8, 16, 32, 64):
        s = jnp.where(jnp.bitwise_and(e, k) != 0, s * 2.0**-k, s)
    return jnp.where(jnp.bitwise_and(e, 128) != 0, (s * 2.0**-64) * 2.0**-64, s)


def pack_columns(words, scales, zeros, blocks, rows):
    parts = [words[:, b * 128 : (b + 1) * 128] for b in range(blocks)]
    parts.append(scales.reshape(blocks, 128))
    parts.append(zeros.reshape(blocks, 128))
    short = rows - 18 * blocks
    if short:
        parts.append(jnp.zeros((short, 128), I32))
    return jnp.concatenate(parts, axis=0)


def permute_kernel(own_ref, other_ref, p_ref, out_ref):
    p = p_ref[...]
    out_ref[:256, :] = jnp.dot(own_ref[...], p, preferred_element_type=F32).astype(BF16)
    out_ref[256:, :] = jnp.dot(other_ref[...], p, preferred_element_type=F32).astype(BF16)


def permute_features(own, other):
    d = np.arange(256)
    source = (d // 64) * 64 + 4 * (d % 16) + (d % 64) // 16
    p = np.zeros((256, 256), np.float32)
    p[source, d] = 1.0
    return pl.pallas_call(
        permute_kernel,
        grid=(16,),
        in_specs=[
            pl.BlockSpec((256, 256), lambda i: (0, i)),
            pl.BlockSpec((256, 256), lambda i: (0, i)),
            pl.BlockSpec((256, 256), lambda i: (0, 0)),
        ],
        out_specs=pl.BlockSpec((512, 256), lambda i: (0, i)),
        out_shape=jax.ShapeDtypeStruct((512, 4096), BF16),
        name="permute_features",
    )(own, other, jnp.asarray(p, BF16))


def dequantize_part(where_ref, refs, weights_ref, first, blocks, rows, x_outer):
    for r, ref in enumerate(refs):

        def one(n, carry, r=r, ref=ref):
            inner, slot = n // 4, n % 4
            outer_at = (where_ref[X if x_outer else Y] + r) % 4
            inner_at = (where_ref[Y if x_outer else X] + inner) % 4
            slot_at = (where_ref[Z] + slot) % 4
            x_at, y_at = (outer_at, inner_at) if x_outer else (inner_at, outer_at)
            row = pl.multiple_of(x_at * 1024 + y_at * 256 + slot_at * 64, 64)
            base = pl.multiple_of(n * rows, 8)
            tail = ref[pl.ds(base + 16 * blocks, rows - 16 * blocks), :]
            scales = decode_scale(tail[:blocks])
            zeros = tail[blocks : 2 * blocks].astype(F32) * (1.0 / 128.0)
            for b in range(blocks):
                words = ref[pl.ds(base + 16 * b, 16), :]
                for i in range(4):
                    code = jnp.bitwise_and(jnp.right_shift(words, 4 * i), 15).astype(F32)
                    value = (code - zeros[b : b + 1]) * scales[b : b + 1]
                    weights_ref[
                        pl.ds(row + 16 * i, 16), first + b * 128 : first + (b + 1) * 128
                    ] = value.astype(BF16)
            return carry

        lax.fori_loop(0, 16, one, 0)


def rope(x, cosine, sine):
    return x * cosine + pltpu.roll(x, 64, 1) * sine


def project_kv_kernel(where_ref, *refs):
    a, b = refs[0:4], refs[4:8]
    x_ref, low_ref, up_ref, cos_ref, sin_ref, out_ref, w_ref = refs[8:]
    dequantize_part(where_ref, a, w_ref, 0, 2, 40, True)
    dequantize_part(where_ref, b, w_ref, 256, 2, 40, False)
    k = jnp.dot(x_ref[...], w_ref[:, 0:256], preferred_element_type=F32).astype(BF16).astype(F32)
    for h in range(2):
        at = slice(h * 128, (h + 1) * 128)
        out_ref[:, at] = rope(k[:, at], cos_ref[...], sin_ref[...]).astype(BF16)
    v = jnp.dot(x_ref[...], w_ref[:, 256:512], preferred_element_type=F32).astype(BF16).astype(F32)
    add = jnp.dot(low_ref[:, 64:128], up_ref[...], preferred_element_type=F32)
    out_ref[:, 256:512] = (v + SCALE * add).astype(BF16)


def project_q_kernel(where_ref, *refs):
    a, b = refs[0:4], refs[4:8]
    x_ref, low_ref, up_ref, cos_ref, sin_ref, out_ref, w_ref = refs[8:]
    dequantize_part(where_ref, a, w_ref, 0, 4, 72, True)
    dequantize_part(where_ref, b, w_ref, 512, 4, 72, False)

    def tile(t, carry):
        col = pl.multiple_of(t * 256, 256)
        q = jnp.dot(x_ref[...], w_ref[:, pl.ds(col, 256)], preferred_element_type=F32)
        q = q.astype(BF16).astype(F32)
        add = jnp.dot(low_ref[:, 0:64], up_ref[:, pl.ds(col, 256)], preferred_element_type=F32)
        q = q + SCALE * add
        for h in range(2):
            out_ref[:, pl.ds(pl.multiple_of(col + h * 128, 128), 128)] = rope(
                q[:, h * 128 : (h + 1) * 128], cos_ref[...], sin_ref[...]
            ).astype(BF16)
        return carry

    lax.fori_loop(0, 4, tile, 0)


def project(kernel, where, a, b, x, low, up, cosine, sine, columns, name):
    full = pl.BlockSpec(memory_space=pltpu.VMEM)
    return pl.pallas_call(
        kernel,
        in_specs=[pl.BlockSpec(memory_space=pltpu.SMEM)] + [full] * 13,
        out_specs=full,
        out_shape=jax.ShapeDtypeStruct((512, columns), BF16),
        scratch_shapes=[pltpu.VMEM((4096, columns), BF16)],
        compiler_params=pltpu.CompilerParams(vmem_limit_bytes=VMEM),
        name=name,
    )(where, *a, *b, x, low, up, cosine, sine)


def attention_kernel(
    piece_ref,
    q_ref,
    g_ref,
    own_ref,
    other_ref,
    start_ref,
    cos_ref,
    sin_ref,
    out_ref,
    dq_ref,
    dv_own_ref,
    dv_other_ref,
    kv_ref,
    dv_ref,
):
    head, step = pl.program_id(0), pl.program_id(1)

    @pl.when((head == 0) & (step == 0))
    def _():
        for n in range(4):
            at = pl.multiple_of(piece_ref[n] * 128, 128)
            kv_ref[pl.ds(at, 128), :] = own_ref[n * 128 : (n + 1) * 128, :]
            at = pl.multiple_of(piece_ref[4 + n] * 128, 128)
            kv_ref[pl.ds(at, 128), :] = other_ref[n * 128 : (n + 1) * 128, :]

    @pl.when(step == 0)
    def _():
        dv_ref[...] = jnp.zeros_like(dv_ref)

    piece = piece_ref[step]
    first = pl.multiple_of(jnp.maximum(piece - 4, 0) * 128, 128)
    k = kv_ref[pl.ds(first, 640), pl.ds(pl.multiple_of(head * 128, 128), 128)]
    v = kv_ref[pl.ds(first, 640), pl.ds(pl.multiple_of(256 + head * 128, 128), 128)]
    q = jnp.concatenate([q_ref[:, i * 128 : (i + 1) * 128] for i in range(4)], axis=0)
    g = jnp.concatenate([g_ref[:, i * 128 : (i + 1) * 128] for i in range(4)], axis=0)
    across = (((1,), (1,)), ((), ()))
    scores = lax.dot_general(q, k, across, preferred_element_type=F32) * ROOT
    key_at = first + lax.broadcasted_iota(I32, (128, 640), 1)
    query_at = piece * 128 + lax.broadcasted_iota(I32, (128, 640), 0)
    allowed = (key_at >= start_ref[...]) & (key_at <= query_at)
    bias = jnp.where(allowed, 0.0, -1e30)
    scores = scores + jnp.concatenate([bias] * 4, axis=0)
    top = jnp.max(scores, axis=-1, keepdims=True)
    e = jnp.exp(scores - top)
    p = e * (1.0 / jnp.sum(e, axis=-1, keepdims=True))
    low = p.astype(BF16)
    out = jnp.dot(low, v, preferred_element_type=F32).astype(BF16)
    dp = lax.dot_general(g, v, across, preferred_element_type=F32)
    row = jnp.sum(p * dp, axis=-1, keepdims=True)
    ds = (p * (dp - row) * ROOT).astype(BF16)
    dq = jnp.dot(ds, k, preferred_element_type=F32)
    dv_ref[pl.ds(first, 640), :] += lax.dot_general(
        low, g, (((0,), (0,)), ((), ())), preferred_element_type=F32
    )
    for i in range(4):
        at = slice(i * 128, (i + 1) * 128)
        out_ref[:, at] = out[at]
        dq_ref[:, at] = rope(dq[at], cos_ref[...], -sin_ref[...]).astype(BF16)

    @pl.when(step == 3)
    def _():
        for n in range(4):
            at = pl.multiple_of(piece_ref[n] * 128, 128)
            dv_own_ref[n * 128 : (n + 1) * 128, :] = dv_ref[pl.ds(at, 128), :]
            at = pl.multiple_of(piece_ref[4 + n] * 128, 128)
            dv_other_ref[n * 128 : (n + 1) * 128, :] = dv_ref[pl.ds(at, 128), :].astype(BF16)


def attend(pieces, q, g, own, other, starts, cosine, sine):
    block = pl.BlockSpec((128, 512), lambda h, s, p: (s, h))
    whole = pl.BlockSpec((512, 512), lambda h, s, p: (0, 0))
    rows = pl.BlockSpec((128, 128), lambda h, s, p: (s, 0))
    head = pl.BlockSpec((512, 128), lambda h, s, p: (0, h))
    return pl.pallas_call(
        attention_kernel,
        grid_spec=pltpu.PrefetchScalarGridSpec(
            num_scalar_prefetch=1,
            grid=(2, 4),
            in_specs=[
                block,
                block,
                whole,
                whole,
                pl.BlockSpec((128, 1), lambda h, s, p: (s, 0)),
                rows,
                rows,
            ],
            out_specs=[block, block, head, head],
            scratch_shapes=[pltpu.VMEM((1024, 512), BF16), pltpu.VMEM((1024, 128), F32)],
        ),
        out_shape=[
            jax.ShapeDtypeStruct((512, 1024), BF16),
            jax.ShapeDtypeStruct((512, 1024), BF16),
            jax.ShapeDtypeStruct((512, 256), F32),
            jax.ShapeDtypeStruct((512, 256), BF16),
        ],
        compiler_params=pltpu.CompilerParams(vmem_limit_bytes=VMEM),
        name="attention",
    )(pieces, q, g, own, other, starts, cosine, sine)


def on_device(hidden, gain, words, scale_zeros, down, query_up, value_up, documents, cotangent):
    f = lax.axis_index("fsdp")
    c = lax.axis_index("ctx")
    x, y, z = f // 16, f // 4 % 4, f % 4
    pair, core = c // 2, c % 2
    where = jnp.stack([x, y, z]).astype(I32)

    with jax.named_scope("pack_words"):
        words, scale_zeros = words[0], scale_zeros[0]
        codes = scale_code(scale_zeros[0:1])
        zero_codes = (scale_zeros[1:2].astype(F32) * 128.0).astype(I32)

        def columns(first, count, rows):
            def cut(array):
                return lax.dynamic_slice_in_dim(array, first, count, 1)

            return pack_columns(cut(words), cut(codes), cut(zero_codes), count // 128, rows)

        packed = jnp.concatenate(
            [
                columns(2048 + core * 256, 256, 40),
                columns(core * 1024, 512, 72),
                columns(2560 + core * 256, 256, 40),
                columns(core * 1024 + 512, 512, 72),
            ],
            axis=0,
        )
    with jax.named_scope("gather_z"):
        slots = gather_axis(packed, Z)

    def cut_slots(first, count):
        return [s[first : first + count] for s in slots]

    with jax.named_scope("gather_inner"):
        part_a = jnp.concatenate(cut_slots(0, 40) + cut_slots(40, 72), axis=0)
        part_b = jnp.concatenate(cut_slots(112, 40) + cut_slots(152, 72), axis=0)
        inner_a = gather_axis(part_a, Y)
        inner_b = gather_axis(part_b, X)
    with jax.named_scope("gather_kv"):
        kv_a = gather_axis(jnp.concatenate([p[:160] for p in inner_a], axis=0), X)
        kv_b = gather_axis(jnp.concatenate([p[:160] for p in inner_b], axis=0), Y)
    with jax.named_scope("gather_q"):
        q_a = gather_axis(jnp.concatenate([p[160:] for p in inner_a], axis=0), X)
        q_b = gather_axis(jnp.concatenate([p[160:] for p in inner_b], axis=0), Y)

    with jax.named_scope("norm"):
        wide = hidden[0].astype(F32)
        mean_square = jnp.mean(wide * wide, axis=-1, keepdims=True)
        normed = (wide * lax.rsqrt(mean_square + EPS) * gain.astype(F32)).astype(BF16)
        normed_other = take_from(normed, CORE, 1)
        permuted = permute_features(normed, normed_other)
    with jax.named_scope("adapter_in"):
        low = jnp.concatenate(
            [
                jnp.dot(n, down, preferred_element_type=F32).astype(BF16)
                for n in (normed, normed_other)
            ],
            axis=0,
        )
    up_q = lax.dynamic_slice_in_dim(query_up, core * 1024, 1024, 1)
    up_v = lax.dynamic_slice_in_dim(value_up, core * 256, 256, 1)
    with jax.named_scope("cotangent_heads"):
        g = cotangent[0]
        g_own = lax.dynamic_slice_in_dim(g, core * 1024, 1024, 1)
        g_other = take_from(lax.dynamic_slice_in_dim(g, (1 - core) * 1024, 1024, 1), CORE, 1)
        g = jnp.concatenate([g_own, g_other], axis=0)

    with jax.named_scope("tables"):
        c_pair = (1 - pair) * 2 + core
        pieces = jnp.stack(
            [
                c,
                7 - c,
                c ^ 1,
                7 - (c ^ 1),
                c_pair,
                7 - c_pair,
                c_pair ^ 1,
                7 - (c_pair ^ 1),
            ]
        ).astype(I32)
        at = (pieces[:4, None] * 128 + jnp.arange(128, dtype=I32)[None, :]).reshape(512)
        angles = at.astype(F32)[:, None] * frequencies()[None, :]
        cosine, sine = jnp.cos(angles), jnp.sin(angles)
        cosine = jnp.concatenate([cosine, cosine], axis=1)
        sine = jnp.concatenate([-sine, sine], axis=1)
        docs = documents[0]
        spot = jnp.arange(1024, dtype=I32)
        fresh = jnp.concatenate([jnp.ones((1,), bool), docs[1:] != docs[:-1]])
        start = lax.cummax(jnp.where(fresh, spot, 0))
        start = start.reshape(8, 128)
        starts = jnp.concatenate(
            [lax.dynamic_slice_in_dim(start, pieces[n], 1, 0) for n in range(4)], axis=0
        ).reshape(512, 1)

    with jax.named_scope("project_kv"):
        kv = project(
            project_kv_kernel, where, kv_a, kv_b, permuted, low, up_v, cosine, sine, 512, "project_kv"
        )
        kv_other = take_from(kv, PAIR, 1)
    with jax.named_scope("project_q"):
        q = project(
            project_q_kernel, where, q_a, q_b, permuted, low, up_q, cosine, sine, 1024, "project_q"
        )
    with jax.named_scope("attention"):
        out, dq, dv_own, dv_other = attend(pieces, q, g, kv, kv_other, starts, cosine, sine)
    with jax.named_scope("context_rows"):
        out_other = take_from(out[256:], CORE, 1)
        context = jnp.concatenate([out[:256], out_other, out[:256]], axis=1)
        context = lax.dynamic_slice_in_dim(context, core * 1024, 2048, 1)[None]
    with jax.named_scope("value_grad"):
        dv = (dv_own + take_from(dv_other, PAIR, 1).astype(F32)).astype(BF16)

    rows_dims = (((0,), (0,)), ((), ()))
    across = (((1,), (1,)), ((), ()))
    with jax.named_scope("adapter_grad"):
        term = jnp.concatenate(
            [
                SCALE * lax.dot_general(dq, up_q, across, preferred_element_type=F32),
                SCALE * lax.dot_general(dv, up_v, across, preferred_element_type=F32),
            ],
            axis=1,
        )
        term_other = take_from(term, CORE, 1)
        low_grad = (term + jnp.concatenate([term_other[256:], term_other[:256]], axis=0)).astype(BF16)
    with jax.named_scope("up_terms"):
        up = jnp.concatenate(
            [
                SCALE * lax.dot_general(low[:, :64], dq, rows_dims, preferred_element_type=F32),
                SCALE * lax.dot_general(low[:, 64:], dv, rows_dims, preferred_element_type=F32),
            ],
            axis=1,
        )
        up = jnp.concatenate([up[:, b * 128 : (b + 1) * 128] for b in range(10)], axis=0)
    with jax.named_scope("down_terms"):
        grad = lax.dot_general(
            normed, low_grad[:256], rows_dims, preferred_element_type=F32
        ) + lax.dot_general(normed_other, low_grad[256:], rows_dims, preferred_element_type=F32)
        grad = lax.dynamic_index_in_dim(grad.reshape(128, 2, 16, 128), core, 1, keepdims=False)
    with jax.named_scope("sum_x"):
        pieces_x = jnp.concatenate([grad.reshape(4, 512, 128), up.reshape(4, 160, 128)], axis=1)
        total = scatter_axis(pieces_x, X, x, narrow=True)
    with jax.named_scope("sum_y"):
        pieces_y = jnp.concatenate(
            [total[:512].reshape(4, 128, 128), total[512:].reshape(4, 40, 128)], axis=1
        )
        total = scatter_axis(pieces_y, Y, y)
    with jax.named_scope("sum_z"):
        pieces_z = jnp.concatenate(
            [total[:128].reshape(4, 32, 128), jnp.broadcast_to(total[None, 128:], (4, 40, 128))],
            axis=1,
        )
        total = scatter_axis(pieces_z, Z, z)
    with jax.named_scope("sum_pair"):
        mine = lax.dynamic_slice_in_dim(total, pair * 16, 16, 0)
        theirs = lax.dynamic_slice_in_dim(total, (1 - pair) * 16, 16, 0)
        got = take_from(jnp.concatenate([theirs, total[32:]], axis=0), PAIR, 1)
        grad_down = mine + got[:16]
        up = total[32:] + got[16:]
    with jax.named_scope("share_up"):
        up = absolute(gather_axis(up, Y), y).reshape(160, 128)
        up = absolute(gather_axis(up, X), x).reshape(640, 128)
        up_other = take_from(up, CORE, 1)
        both = jnp.stack([up, up_other, up])
        both = lax.dynamic_slice_in_dim(both, core, 2, 0).reshape(2, 10, 64, 128)
        query_up_gradient = jnp.transpose(both[:, :8], (2, 0, 1, 3)).reshape(64, 2048)
        value_up_gradient = jnp.transpose(both[:, 8:], (2, 0, 1, 3)).reshape(64, 512)
    return context, grad_down, query_up_gradient, value_up_gradient


def solution(mesh):
    return jax.shard_map(
        on_device,
        mesh=mesh,
        in_specs=(
            P("fsdp", "ctx", None),
            P(),
            P("fsdp", None, None),
            P("fsdp", None, None),
            P(),
            P(),
            P(),
            P("fsdp", None),
            P("fsdp", "ctx", None),
        ),
        out_specs=(P("fsdp", "ctx", None), P(("fsdp", "ctx"), None), P(), P()),
        check_vma=False,
    )
```

```python
import functools
import math

import jax
import jax.numpy as jnp
import numpy as np
from jax import lax
from jax.experimental import pallas as pl
from jax.experimental.pallas import tpu as pltpu
from jax.sharding import PartitionSpec as P

HEAD = 128
SCALE = 0.25
EPS = 1e-05
THETA = 500000.0
ROOT = 1.0 / math.sqrt(HEAD)
AXES = ("fsdp", "ctx")
VMEM = 60 * 1024 * 1024
F32, BF16, I32 = jnp.float32, jnp.bfloat16, jnp.int32


def place(l):
    f, c = divmod(l, 4)
    return [f // 16, f // 4 % 4, f % 4, c // 2, c % 2]


def index(p):
    return ((p[0] * 4 + p[1]) * 4 + p[2]) * 4 + p[3] * 2 + p[4]


SIZES = (4, 4, 4, 2, 2)
X, Y, Z, PAIR, CORE = range(5)


def take_from(value, axis, step):
    pairs = []
    for l in range(256):
        p = place(l)
        p[axis] = (p[axis] - step) % SIZES[axis]
        pairs.append((l, index(p)))
    return lax.ppermute(value, AXES, pairs)


def gather_axis(value, axis):
    return [value] + [take_from(value, axis, r) for r in (1, 2, 3)]


def absolute(parts, coordinate):
    twice = jnp.stack(parts + parts)
    return lax.dynamic_slice_in_dim(twice, (4 - coordinate) % 4, 4, 0)


def scatter_axis(pieces, axis, coordinate, narrow=False):
    own = lax.dynamic_index_in_dim(pieces, coordinate, 0, keepdims=False)
    sent = pieces.astype(BF16) if narrow else pieces
    got = [
        take_from(
            lax.dynamic_index_in_dim(sent, (coordinate + 4 - r) % 4, 0, keepdims=False), axis, r
        )
        for r in (1, 2, 3)
    ]
    return own + got[0].astype(F32) + got[1].astype(F32) + got[2].astype(F32)


def frequencies():
    exponent = jnp.arange(0, HEAD, 2, dtype=F32) / HEAD
    inverse = 1.0 / THETA**exponent
    wavelength = 2.0 * math.pi / inverse
    blend = (8192.0 / wavelength - 1.0) / 3.0
    middle = (1.0 - blend) * inverse / 8.0 + blend * inverse
    return jnp.where(
        wavelength < 2048.0, inverse, jnp.where(wavelength > 8192.0, inverse / 8.0, middle)
    )


def scale_code(scale):
    m = scale.astype(F32) * 16.0
    e = jnp.full(m.shape, 4, I32)
    for k in (64, 64, 32, 16, 8, 4, 2, 1):
        small = m < 2.0 ** (8 - k)
        m = jnp.where(small, m * 2.0**k, m)
        e = jnp.where(small, e + k, e)
    return m.astype(I32) + 256 * e


def decode_scale(code):
    s = jnp.bitwise_and(code, 255).astype(F32)
    e = jnp.right_shift(code, 8)
    for k in (1, 2, 4, 8, 16, 32, 64):
        s = jnp.where(jnp.bitwise_and(e, k) != 0, s * 2.0**-k, s)
    return jnp.where(jnp.bitwise_and(e, 128) != 0, (s * 2.0**-64) * 2.0**-64, s)


def pack_columns(words, scales, zeros, blocks, rows):
    parts = [words[:, b * 128 : (b + 1) * 128] for b in range(blocks)]
    parts.append(scales.reshape(blocks, 128))
    parts.append(zeros.reshape(blocks, 128))
    short = rows - 18 * blocks
    if short:
        parts.append(jnp.zeros((short, 128), I32))
    return jnp.concatenate(parts, axis=0)


def cost(flops, moved):
    return pl.CostEstimate(flops=int(flops), bytes_accessed=int(moved), transcendentals=0)


def permute_kernel(own_ref, other_ref, p_ref, out_ref):
    p = p_ref[...]
    for n in range(4):
        at = slice(n * 256, (n + 1) * 256)
        out_ref[:256, at] = jnp.dot(own_ref[:, at], p, preferred_element_type=F32).astype(BF16)
        out_ref[256:, at] = jnp.dot(other_ref[:, at], p, preferred_element_type=F32).astype(BF16)


def permute_features(own, other):
    d = np.arange(256)
    source = (d // 64) * 64 + 4 * (d % 16) + (d % 64) // 16
    p = np.zeros((256, 256), np.float32)
    p[source, d] = 1.0
    return pl.pallas_call(
        permute_kernel,
        grid=(4,),
        in_specs=[
            pl.BlockSpec((256, 1024), lambda i: (0, i)),
            pl.BlockSpec((256, 1024), lambda i: (0, i)),
            pl.BlockSpec((256, 256), lambda i: (0, 0)),
        ],
        out_specs=pl.BlockSpec((512, 1024), lambda i: (0, i)),
        cost_estimate=cost(1.1e9, 8.4e6),
        out_shape=jax.ShapeDtypeStruct((512, 4096), BF16),
        name="permute_features",
    )(own, other, jnp.asarray(p, BF16))


def join_kernel(cuts, *refs):
    ins, outs = refs[: len(refs) - len(cuts)], refs[len(refs) - len(cuts) :]
    for out, (first, count) in zip(outs, cuts):
        for n, ref in enumerate(ins):
            out[n * count : (n + 1) * count, :] = ref[first : first + count, :]


def join(parts, cuts, name):
    full = pl.BlockSpec(memory_space=pltpu.VMEM)
    return pl.pallas_call(
        functools.partial(join_kernel, cuts),
        in_specs=[full] * len(parts),
        out_specs=[full] * len(cuts),
        out_shape=[jax.ShapeDtypeStruct((len(parts) * n, 128), I32) for _, n in cuts],
        cost_estimate=cost(0, 4e6),
        name=name,
    )(*parts)


def dequantize(where_ref, ref, scale_ref, weights_ref, outer, inner_axis, blocks, rows):
    last = 16 * blocks
    codes = jnp.concatenate([ref[n * rows + last : (n + 1) * rows, :] for n in range(16)], axis=0)
    pad = rows - last
    row_kind = jnp.bitwise_and(lax.broadcasted_iota(I32, codes.shape, 0), pad - 1)
    scale_ref[: 16 * pad, :] = jnp.where(
        row_kind < blocks, decode_scale(codes), codes.astype(F32) * (1.0 / 128.0)
    )

    def one(n, carry):
        inner_at = (where_ref[inner_axis] + n // 4) % 4
        slot_at = (where_ref[Z] + n % 4) % 4
        row = pl.multiple_of(outer + inner_at * 256 + slot_at * 64, 64)
        base = pl.multiple_of(n * rows, 8)
        tail = scale_ref[pl.ds(pl.multiple_of(n * pad, 8), pad), :]
        for b in range(blocks):
            words = ref[pl.ds(base + 16 * b, 16), :]
            scale = jnp.broadcast_to(tail[b : b + 1], (16, 128))
            zero = jnp.broadcast_to(tail[blocks + b : blocks + b + 1], (16, 128))
            for i in range(4):
                code = jnp.bitwise_and(jnp.right_shift(words, 4 * i), 15).astype(F32)
                weights_ref[pl.ds(row + 16 * i, 16), b * 128 : (b + 1) * 128] = (
                    (code - zero) * scale
                ).astype(BF16)
        return carry

    lax.fori_loop(0, 16, one, 0, unroll=2)


def rope(x, cosine, sine):
    return x * cosine + pltpu.roll(x, 64, 1) * sine


def partial_products(where_ref, r, a_ref, b_ref, x_ref, scale_ref, w_ref, blocks, rows):
    x_at = (where_ref[X] + r) % 4
    y_at = (where_ref[Y] + r) % 4
    dequantize(where_ref, a_ref, scale_ref, w_ref, 0, Y, blocks, rows)
    strip = x_ref[:, pl.ds(pl.multiple_of(x_at * 1024, 1024), 1024)]
    first = jnp.dot(strip, w_ref[:1024, :], preferred_element_type=F32)
    dequantize(where_ref, b_ref, scale_ref, w_ref, 1024, X, blocks, rows)
    strip = jnp.concatenate(
        [x_ref[:, pl.ds(pl.multiple_of(n * 1024 + y_at * 256, 256), 256)] for n in range(4)], axis=1
    )
    return first, jnp.dot(strip, w_ref[1024:, :], preferred_element_type=F32)


def project_kv_kernel(where_ref, *refs):
    a, b = refs[0:4], refs[4:8]
    x_ref, low_ref, up_ref, cos_ref, sin_ref, out_ref, scale_ref, w_ref = refs[8:]
    k = v = 0.0
    for r in range(4):
        more = partial_products(where_ref, r, a[r], b[r], x_ref, scale_ref, w_ref, 2, 40)
        k, v = k + more[0], v + more[1]
    k = k.astype(BF16).astype(F32)
    for h in range(2):
        at = slice(h * 128, (h + 1) * 128)
        out_ref[:, at] = rope(k[:, at], cos_ref[...], sin_ref[...]).astype(BF16)
    v = v.astype(BF16).astype(F32)
    add = jnp.dot(low_ref[:, 64:128], up_ref[...], preferred_element_type=F32)
    out_ref[:, 256:512] = (v + SCALE * add).astype(BF16)


def project_kv(where, a, b, x, low, up, cosine, sine):
    full = pl.BlockSpec(memory_space=pltpu.VMEM)
    return pl.pallas_call(
        project_kv_kernel,
        in_specs=[pl.BlockSpec(memory_space=pltpu.SMEM)] + [full] * 13,
        out_specs=full,
        out_shape=jax.ShapeDtypeStruct((512, 512), BF16),
        scratch_shapes=[pltpu.VMEM((128, 128), F32), pltpu.VMEM((2048, 256), BF16)],
        compiler_params=pltpu.CompilerParams(vmem_limit_bytes=VMEM),
        cost_estimate=cost(6e9, 8e6),
        name="project_kv",
    )(where, *a, *b, x, low, up, cosine, sine)


def project_q_kernel(r, first, last, where_ref, a_ref, b_ref, x_ref, *refs):
    scale_ref, w_ref = refs[-2:]
    more = partial_products(where_ref, r, a_ref, b_ref, x_ref, scale_ref, w_ref, 4, 72)
    if not first:
        sum_ref = refs[0]
        more = sum_ref[:, :512] + more[0], sum_ref[:, 512:] + more[1]
    if not last:
        out_ref = refs[-3]
        out_ref[:, :512] = more[0]
        out_ref[:, 512:] = more[1]
        return
    low_ref, up_ref, cos_ref, sin_ref, out_ref = refs[1:6]
    add = jnp.dot(low_ref[:, 0:64], up_ref[...], preferred_element_type=F32)
    for n in range(8):
        at = slice(n % 4 * 128, (n % 4 + 1) * 128)
        q = more[n // 4][:, at].astype(BF16).astype(F32) + SCALE * add[:, n * 128 : (n + 1) * 128]
        out_ref[:, n * 128 : (n + 1) * 128] = rope(q, cos_ref[...], sin_ref[...]).astype(BF16)


def project_q(r, where, a, b, x, total, rest):
    first, last = total is None, len(rest) > 0
    more = ([] if first else [total]) + list(rest)
    full = pl.BlockSpec(memory_space=pltpu.VMEM)
    return pl.pallas_call(
        functools.partial(project_q_kernel, r, first, last),
        in_specs=[pl.BlockSpec(memory_space=pltpu.SMEM)] + [full] * (3 + len(more)),
        out_specs=full,
        out_shape=jax.ShapeDtypeStruct((512, 1024), BF16 if last else F32),
        scratch_shapes=[pltpu.VMEM((128, 128), F32), pltpu.VMEM((2048, 512), BF16)],
        compiler_params=pltpu.CompilerParams(vmem_limit_bytes=VMEM),
        cost_estimate=cost(3e9, 8e6),
        name="project_q",
    )(where, a, b, x, *more)


def attention_kernel(
    piece_ref,
    q_ref,
    g_ref,
    own_ref,
    other_ref,
    start_ref,
    cos_ref,
    sin_ref,
    out_ref,
    dq_ref,
    dv_own_ref,
    dv_other_ref,
    kv_ref,
    dv_ref,
):
    head, step = pl.program_id(0), pl.program_id(1)

    @pl.when((head == 0) & (step == 0))
    def _():
        for n in range(4):
            at = pl.multiple_of(piece_ref[n] * 128, 128)
            kv_ref[pl.ds(at, 128), :] = own_ref[n * 128 : (n + 1) * 128, :]
            at = pl.multiple_of(piece_ref[4 + n] * 128, 128)
            kv_ref[pl.ds(at, 128), :] = other_ref[n * 128 : (n + 1) * 128, :]

    @pl.when(step == 0)
    def _():
        dv_ref[...] = jnp.zeros_like(dv_ref)

    piece = piece_ref[step]
    first = pl.multiple_of(jnp.maximum(piece - 4, 0) * 128, 128)
    k = kv_ref[pl.ds(first, 640), pl.ds(pl.multiple_of(head * 128, 128), 128)]
    v = kv_ref[pl.ds(first, 640), pl.ds(pl.multiple_of(256 + head * 128, 128), 128)]
    q = jnp.concatenate([q_ref[:, i * 128 : (i + 1) * 128] for i in range(4)], axis=0)
    g = jnp.concatenate([g_ref[:, i * 128 : (i + 1) * 128] for i in range(4)], axis=0)
    across = (((1,), (1,)), ((), ()))
    scores = lax.dot_general(q, k, across, preferred_element_type=F32) * ROOT
    key_at = first + lax.broadcasted_iota(I32, (128, 640), 1)
    query_at = piece * 128 + lax.broadcasted_iota(I32, (128, 640), 0)
    allowed = (key_at >= start_ref[...]) & (key_at <= query_at)
    bias = jnp.where(allowed, 0.0, -1e30)
    scores = scores + jnp.concatenate([bias] * 4, axis=0)
    top = jnp.max(scores, axis=-1, keepdims=True)
    e = jnp.exp(scores - top)
    p = e * (1.0 / jnp.sum(e, axis=-1, keepdims=True))
    low = p.astype(BF16)
    out = jnp.dot(low, v, preferred_element_type=F32).astype(BF16)
    dp = lax.dot_general(g, v, across, preferred_element_type=F32)
    row = jnp.sum(p * dp, axis=-1, keepdims=True)
    ds = (p * (dp - row) * ROOT).astype(BF16)
    dq = jnp.dot(ds, k, preferred_element_type=F32)
    dv_ref[pl.ds(first, 640), :] += lax.dot_general(
        low, g, (((0,), (0,)), ((), ())), preferred_element_type=F32
    )
    for i in range(4):
        at = slice(i * 128, (i + 1) * 128)
        out_ref[:, at] = out[at]
        dq_ref[:, at] = rope(dq[at], cos_ref[...], -sin_ref[...]).astype(BF16)

    @pl.when(step == 3)
    def _():
        for n in range(4):
            at = pl.multiple_of(piece_ref[n] * 128, 128)
            dv_own_ref[n * 128 : (n + 1) * 128, :] = dv_ref[pl.ds(at, 128), :]
            at = pl.multiple_of(piece_ref[4 + n] * 128, 128)
            dv_other_ref[n * 128 : (n + 1) * 128, :] = dv_ref[pl.ds(at, 128), :].astype(BF16)


def attend(pieces, q, g, own, other, starts, cosine, sine):
    block = pl.BlockSpec((128, 512), lambda h, s, p: (s, h))
    whole = pl.BlockSpec((512, 512), lambda h, s, p: (0, 0))
    rows = pl.BlockSpec((128, 128), lambda h, s, p: (s, 0))
    head = pl.BlockSpec((512, 128), lambda h, s, p: (0, h))
    return pl.pallas_call(
        attention_kernel,
        grid_spec=pltpu.PrefetchScalarGridSpec(
            num_scalar_prefetch=1,
            grid=(2, 4),
            in_specs=[
                block,
                block,
                whole,
                whole,
                pl.BlockSpec((128, 1), lambda h, s, p: (s, 0)),
                rows,
                rows,
            ],
            out_specs=[block, block, head, head],
            scratch_shapes=[pltpu.VMEM((1024, 512), BF16), pltpu.VMEM((1024, 128), F32)],
        ),
        out_shape=[
            jax.ShapeDtypeStruct((512, 1024), BF16),
            jax.ShapeDtypeStruct((512, 1024), BF16),
            jax.ShapeDtypeStruct((512, 256), F32),
            jax.ShapeDtypeStruct((512, 256), BF16),
        ],
        compiler_params=pltpu.CompilerParams(vmem_limit_bytes=VMEM),
        name="attention",
    )(pieces, q, g, own, other, starts, cosine, sine)


def on_device(hidden, gain, words, scale_zeros, down, query_up, value_up, documents, cotangent):
    f = lax.axis_index("fsdp")
    c = lax.axis_index("ctx")
    x, y, z = f // 16, f // 4 % 4, f % 4
    pair, core = c // 2, c % 2
    where = jnp.stack([x, y, z]).astype(I32)

    with jax.named_scope("pack_words"):
        words, scale_zeros = words[0], scale_zeros[0]
        codes = scale_code(scale_zeros[0:1])
        zero_codes = (scale_zeros[1:2].astype(F32) * 128.0).astype(I32)

        def columns(first, count, rows):
            def cut(array):
                return lax.dynamic_slice_in_dim(array, first, count, 1)

            return pack_columns(cut(words), cut(codes), cut(zero_codes), count // 128, rows)

        packed = jnp.concatenate(
            [
                columns(2048 + core * 256, 256, 40),
                columns(core * 1024, 512, 72),
                columns(2560 + core * 256, 256, 40),
                columns(core * 1024 + 512, 512, 72),
            ],
            axis=0,
        )
    with jax.named_scope("gather_z"):
        slots = gather_axis(packed, Z)

    with jax.named_scope("gather_inner"):
        cuts = ((0, 40), (40, 72), (112, 40), (152, 72))
        kv_a, q_a, kv_b, q_b = join(slots, cuts, "join_z")
        kv_a, q_a = gather_axis(kv_a, Y), gather_axis(q_a, Y)
        kv_b, q_b = gather_axis(kv_b, X), gather_axis(q_b, X)
    with jax.named_scope("gather_kv"):
        kv_a = gather_axis(join(kv_a, ((0, 160),), "join_kv_y")[0], X)
        kv_b = gather_axis(join(kv_b, ((0, 160),), "join_kv_x")[0], Y)
    with jax.named_scope("gather_q"):
        q_a = gather_axis(join(q_a, ((0, 288),), "join_q_y")[0], X)
        q_b = gather_axis(join(q_b, ((0, 288),), "join_q_x")[0], Y)

    with jax.named_scope("norm"):
        wide = hidden[0].astype(F32)
        mean_square = jnp.mean(wide * wide, axis=-1, keepdims=True)
        normed = (wide * lax.rsqrt(mean_square + EPS) * gain.astype(F32)).astype(BF16)
        normed_other = take_from(normed, CORE, 1)
        permuted = permute_features(normed, normed_other)
    with jax.named_scope("adapter_in"):
        low = jnp.concatenate(
            [
                jnp.dot(n, down, preferred_element_type=F32).astype(BF16)
                for n in (normed, normed_other)
            ],
            axis=0,
        )
    up_q = lax.dynamic_slice_in_dim(query_up, core * 1024, 1024, 1)
    up_v = lax.dynamic_slice_in_dim(value_up, core * 256, 256, 1)
    with jax.named_scope("cotangent_heads"):
        g = cotangent[0]
        g_own = lax.dynamic_slice_in_dim(g, core * 1024, 1024, 1)
        g_other = take_from(lax.dynamic_slice_in_dim(g, (1 - core) * 1024, 1024, 1), CORE, 1)
        g = jnp.concatenate([g_own, g_other], axis=0)

    with jax.named_scope("tables"):
        c_pair = (1 - pair) * 2 + core
        pieces = jnp.stack(
            [
                c,
                7 - c,
                c ^ 1,
                7 - (c ^ 1),
                c_pair,
                7 - c_pair,
                c_pair ^ 1,
                7 - (c_pair ^ 1),
            ]
        ).astype(I32)
        at = (pieces[:4, None] * 128 + jnp.arange(128, dtype=I32)[None, :]).reshape(512)
        angles = at.astype(F32)[:, None] * frequencies()[None, :]
        cosine, sine = jnp.cos(angles), jnp.sin(angles)
        cosine = jnp.concatenate([cosine, cosine], axis=1)
        sine = jnp.concatenate([-sine, sine], axis=1)
        docs = documents[0]
        spot = jnp.arange(1024, dtype=I32)
        fresh = jnp.concatenate([jnp.ones((1,), bool), docs[1:] != docs[:-1]])
        start = lax.cummax(jnp.where(fresh, spot, 0))
        start = start.reshape(8, 128)
        starts = jnp.concatenate(
            [lax.dynamic_slice_in_dim(start, pieces[n], 1, 0) for n in range(4)], axis=0
        ).reshape(512, 1)

    with jax.named_scope("project_kv"):
        kv = project_kv(where, kv_a, kv_b, permuted, low, up_v, cosine, sine)
        kv_other = take_from(kv, PAIR, 1)
    with jax.named_scope("project_q"):
        q = None
        for r in (0, 1, 3, 2):
            rest = (low, up_q, cosine, sine) if r == 2 else ()
            q = project_q(r, where, q_a[r], q_b[r], permuted, q, rest)
    with jax.named_scope("attention"):
        out, dq, dv_own, dv_other = attend(pieces, q, g, kv, kv_other, starts, cosine, sine)
    with jax.named_scope("context_rows"):
        out_other = take_from(out[256:], CORE, 1)
        context = jnp.concatenate([out[:256], out_other, out[:256]], axis=1)
        context = lax.dynamic_slice_in_dim(context, core * 1024, 2048, 1)[None]
    with jax.named_scope("value_grad"):
        dv = (dv_own + take_from(dv_other, PAIR, 1).astype(F32)).astype(BF16)

    rows_dims = (((0,), (0,)), ((), ()))
    across = (((1,), (1,)), ((), ()))
    with jax.named_scope("adapter_grad"):
        term = jnp.concatenate(
            [
                SCALE * lax.dot_general(dq, up_q, across, preferred_element_type=F32),
                SCALE * lax.dot_general(dv, up_v, across, preferred_element_type=F32),
            ],
            axis=1,
        )
        term_other = take_from(term, CORE, 1)
        low_grad = (term + jnp.concatenate([term_other[256:], term_other[:256]], axis=0)).astype(BF16)
    with jax.named_scope("up_terms"):
        up = jnp.concatenate(
            [
                SCALE * lax.dot_general(low[:, :64], dq, rows_dims, preferred_element_type=F32),
                SCALE * lax.dot_general(low[:, 64:], dv, rows_dims, preferred_element_type=F32),
            ],
            axis=1,
        )
        up = jnp.concatenate([up[:, b * 128 : (b + 1) * 128] for b in range(10)], axis=0)
    with jax.named_scope("down_terms"):
        grad = lax.dot_general(
            normed, low_grad[:256], rows_dims, preferred_element_type=F32
        ) + lax.dot_general(normed_other, low_grad[256:], rows_dims, preferred_element_type=F32)
        grad = lax.dynamic_index_in_dim(grad.reshape(128, 2, 16, 128), core, 1, keepdims=False)
    with jax.named_scope("sum_x"):
        pieces_x = jnp.concatenate([grad.reshape(4, 512, 128), up.reshape(4, 160, 128)], axis=1)
        total = scatter_axis(pieces_x, X, x, narrow=True)
    with jax.named_scope("sum_y"):
        pieces_y = jnp.concatenate(
            [total[:512].reshape(4, 128, 128), total[512:].reshape(4, 40, 128)], axis=1
        )
        total = scatter_axis(pieces_y, Y, y)
    with jax.named_scope("sum_z"):
        pieces_z = jnp.concatenate(
            [total[:128].reshape(4, 32, 128), jnp.broadcast_to(total[None, 128:], (4, 40, 128))],
            axis=1,
        )
        total = scatter_axis(pieces_z, Z, z)
    with jax.named_scope("sum_pair"):
        mine = lax.dynamic_slice_in_dim(total, pair * 16, 16, 0)
        theirs = lax.dynamic_slice_in_dim(total, (1 - pair) * 16, 16, 0)
        got = take_from(jnp.concatenate([theirs, total[32:]], axis=0), PAIR, 1)
        grad_down = mine + got[:16]
        up = total[32:] + got[16:]
    with jax.named_scope("share_up"):
        up = absolute(gather_axis(up, Y), y).reshape(160, 128)
        up = absolute(gather_axis(up, X), x).reshape(640, 128)
        up_other = take_from(up, CORE, 1)
        both = jnp.stack([up, up_other, up])
        both = lax.dynamic_slice_in_dim(both, core, 2, 0).reshape(2, 10, 64, 128)
        query_up_gradient = jnp.transpose(both[:, :8], (2, 0, 1, 3)).reshape(64, 2048)
        value_up_gradient = jnp.transpose(both[:, 8:], (2, 0, 1, 3)).reshape(64, 512)
    return context, grad_down, query_up_gradient, value_up_gradient


def solution(mesh):
    return jax.shard_map(
        on_device,
        mesh=mesh,
        in_specs=(
            P("fsdp", "ctx", None),
            P(),
            P("fsdp", None, None),
            P("fsdp", None, None),
            P(),
            P(),
            P(),
            P("fsdp", None),
            P("fsdp", "ctx", None),
        ),
        out_specs=(P("fsdp", "ctx", None), P(("fsdp", "ctx"), None), P(), P()),
        check_vma=False,
    )
```

```python
import functools
import math

import jax
import jax.numpy as jnp
import numpy as np
from jax import lax
from jax.experimental import pallas as pl
from jax.experimental.pallas import tpu as pltpu
from jax.sharding import PartitionSpec as P

HEAD = 128
SCALE = 0.25
EPS = 1e-05
THETA = 500000.0
ROOT = 1.0 / math.sqrt(HEAD)
AXES = ("fsdp", "ctx")
VMEM = 60 * 1024 * 1024
F32, BF16, I32 = jnp.float32, jnp.bfloat16, jnp.int32


def place(l):
    f, c = divmod(l, 4)
    return [f // 16, f // 4 % 4, f % 4, c // 2, c % 2]


def index(p):
    return ((p[0] * 4 + p[1]) * 4 + p[2]) * 4 + p[3] * 2 + p[4]


SIZES = (4, 4, 4, 2, 2)
X, Y, Z, PAIR, CORE = range(5)


def take_from(value, axis, step):
    pairs = []
    for l in range(256):
        p = place(l)
        p[axis] = (p[axis] - step) % SIZES[axis]
        pairs.append((l, index(p)))
    return lax.ppermute(value, AXES, pairs)


def gather_axis(value, axis):
    return [value] + [take_from(value, axis, r) for r in (1, 2, 3)]


PLANE = [[4 * n + z for n in range(16)] for z in range(4)]
COLUMN = [
    [index((x, y, z, pair, core)) for z in range(4) for pair in range(2)]
    for x in range(4)
    for y in range(4)
    for core in range(2)
]


def exchange(parts, groups, axes):
    return lax.all_to_all(parts, axes, 0, 0, tiled=True, axis_index_groups=groups)


def frequencies():
    exponent = jnp.arange(0, HEAD, 2, dtype=F32) / HEAD
    inverse = 1.0 / THETA**exponent
    wavelength = 2.0 * math.pi / inverse
    blend = (8192.0 / wavelength - 1.0) / 3.0
    middle = (1.0 - blend) * inverse / 8.0 + blend * inverse
    return jnp.where(
        wavelength < 2048.0, inverse, jnp.where(wavelength > 8192.0, inverse / 8.0, middle)
    )


def scale_code(scale):
    m = scale.astype(F32) * 16.0
    e = jnp.full(m.shape, 4, I32)
    for k in (64, 64, 32, 16, 8, 4, 2, 1):
        small = m < 2.0 ** (8 - k)
        m = jnp.where(small, m * 2.0**k, m)
        e = jnp.where(small, e + k, e)
    return m.astype(I32) + 256 * e


def decode_scale(code):
    s = jnp.bitwise_and(code, 255).astype(F32)
    e = jnp.right_shift(code, 8)
    for k in (1, 2, 4, 8, 16, 32, 64):
        s = jnp.where(jnp.bitwise_and(e, k) != 0, s * 2.0**-k, s)
    return jnp.where(jnp.bitwise_and(e, 128) != 0, (s * 2.0**-64) * 2.0**-64, s)


def cost(flops, moved):
    return pl.CostEstimate(flops=int(flops), bytes_accessed=int(moved), transcendentals=0)


def pack_kernel(core_ref, words_ref, params_ref, out_ref):
    core = core_ref[0]
    row = 0
    for first, step, blocks, pad in (
        (2048, 256, 2, 4),
        (0, 1024, 4, 0),
        (2560, 256, 2, 4),
        (512, 1024, 4, 0),
    ):
        for b in range(blocks):
            at = pl.ds(pl.multiple_of(first + core * step + b * 128, 128), 128)
            out_ref[row + 16 * b : row + 16 * b + 16, :] = words_ref[0, :, at]
            params = params_ref[0, :, at].astype(F32)
            tail = row + 16 * blocks + b
            out_ref[tail : tail + 1, :] = scale_code(params[0:1])
            out_ref[tail + blocks : tail + blocks + 1, :] = (params[1:2] * 128.0).astype(I32)
        row += 18 * blocks
        if pad:
            out_ref[row : row + pad, :] = jnp.zeros((pad, 128), I32)
            row += pad


def pack(core, words, params):
    full = pl.BlockSpec(memory_space=pltpu.VMEM)
    return pl.pallas_call(
        pack_kernel,
        in_specs=[pl.BlockSpec(memory_space=pltpu.SMEM), full, full],
        out_specs=full,
        out_shape=jax.ShapeDtypeStruct((224, 128), I32),
        name="pack_words",
    )(core, words, params)


def permute_kernel(own_ref, other_ref, p_ref, out_ref):
    p = p_ref[...]
    for n in range(4):
        at = slice(n * 256, (n + 1) * 256)
        out_ref[:256, at] = jnp.dot(own_ref[:, at], p, preferred_element_type=F32).astype(BF16)
        out_ref[256:, at] = jnp.dot(other_ref[:, at], p, preferred_element_type=F32).astype(BF16)


def permute_features(own, other):
    d = np.arange(256)
    source = (d // 64) * 64 + 4 * (d % 16) + (d % 64) // 16
    p = np.zeros((256, 256), np.float32)
    p[source, d] = 1.0
    return pl.pallas_call(
        permute_kernel,
        grid=(4,),
        in_specs=[
            pl.BlockSpec((256, 1024), lambda i: (0, i)),
            pl.BlockSpec((256, 1024), lambda i: (0, i)),
            pl.BlockSpec((256, 256), lambda i: (0, 0)),
        ],
        out_specs=pl.BlockSpec((512, 1024), lambda i: (0, i)),
        cost_estimate=cost(1.1e9, 8.4e6),
        out_shape=jax.ShapeDtypeStruct((512, 4096), BF16),
        name="permute_features",
    )(own, other, jnp.asarray(p, BF16))


def join_kernel(cuts, *refs):
    ins, outs = refs[: len(refs) - len(cuts)], refs[len(refs) - len(cuts) :]
    for out, (first, count) in zip(outs, cuts):
        for n, ref in enumerate(ins):
            out[n * count : (n + 1) * count, :] = ref[first : first + count, :]


def join(parts, cuts, name):
    full = pl.BlockSpec(memory_space=pltpu.VMEM)
    return pl.pallas_call(
        functools.partial(join_kernel, cuts),
        in_specs=[full] * len(parts),
        out_specs=[full] * len(cuts),
        out_shape=[jax.ShapeDtypeStruct((len(parts) * n, 128), I32) for _, n in cuts],
        cost_estimate=cost(0, 4e6),
        name=name,
    )(*parts)


def join_parts_kernel(*refs):
    ins, outs = refs[:4], refs[4:]
    for half, out in enumerate(outs):
        for n, ref in enumerate(ins):
            at = half * 112
            out[n * 40 : (n + 1) * 40, :] = ref[at : at + 40, :]
            out[160 + n * 72 : 160 + (n + 1) * 72, :] = ref[at + 40 : at + 112, :]


def join_parts(slots):
    full = pl.BlockSpec(memory_space=pltpu.VMEM)
    return pl.pallas_call(
        join_parts_kernel,
        in_specs=[full] * 4,
        out_specs=[full] * 2,
        out_shape=[jax.ShapeDtypeStruct((448, 128), I32)] * 2,
        cost_estimate=cost(0, 1e6),
        name="join_z",
    )(*slots)


def dequantize(where_ref, ref, scale_ref, weights_ref, outer, inner_axis, blocks, rows):
    last = 16 * blocks
    codes = jnp.concatenate([ref[n * rows + last : (n + 1) * rows, :] for n in range(16)], axis=0)
    pad = rows - last
    row_kind = jnp.bitwise_and(lax.broadcasted_iota(I32, codes.shape, 0), pad - 1)
    scale_ref[: 16 * pad, :] = jnp.where(
        row_kind < blocks, decode_scale(codes), codes.astype(F32) * (1.0 / 128.0)
    )

    def one(n, carry):
        inner_at = (where_ref[inner_axis] + n // 4) % 4
        slot_at = (where_ref[Z] + n % 4) % 4
        row = pl.multiple_of(outer + inner_at * 256 + slot_at * 64, 64)
        base = pl.multiple_of(n * rows, 8)
        tail = scale_ref[pl.ds(pl.multiple_of(n * pad, 8), pad), :]
        for b in range(blocks):
            words = ref[pl.ds(base + 16 * b, 16), :]
            scale = jnp.broadcast_to(tail[b : b + 1], (16, 128))
            zero = jnp.broadcast_to(tail[blocks + b : blocks + b + 1], (16, 128))
            for i in range(4):
                code = jnp.bitwise_and(jnp.right_shift(words, 4 * i), 15).astype(F32)
                weights_ref[pl.ds(row + 16 * i, 16), b * 128 : (b + 1) * 128] = (
                    (code - zero) * scale
                ).astype(BF16)
        return carry

    lax.fori_loop(0, 16, one, 0, unroll=2)


def rope(x, cosine, sine):
    return x * cosine + pltpu.roll(x, 64, 1) * sine


class Inputs:
    def __init__(self, sources, buffers, semaphores):
        self.buffers, self.copies = buffers, []
        for n, source in enumerate(sources):
            copy = pltpu.make_async_copy(source, buffers[n], semaphores.at[n])
            copy.start()
            self.copies.append(copy)

    def take(self, n):
        if self.copies[n] is not None:
            self.copies[n].wait()
            self.copies[n] = None
        return self.buffers[n]


def product_a(where_ref, r, words, inputs, scale_ref, w_ref, blocks, rows):
    at = (where_ref[X] + r) % 4
    dequantize(where_ref, words, scale_ref, w_ref, 0, Y, blocks, rows)
    strip = inputs.take(0)[:, pl.ds(pl.multiple_of(at * 1024, 1024), 1024)]
    return jnp.dot(strip, w_ref[:, : 128 * blocks], preferred_element_type=F32)


def product_b(where_ref, r, words, inputs, scale_ref, w_ref, blocks, rows):
    at = (where_ref[Y] + r) % 4
    dequantize(where_ref, words, scale_ref, w_ref, 0, X, blocks, rows)
    x_ref = inputs.take(0)
    strip = jnp.concatenate(
        [x_ref[:, pl.ds(pl.multiple_of(n * 1024 + at * 256, 256), 256)] for n in range(4)], axis=1
    )
    return jnp.dot(strip, w_ref[:, : 128 * blocks], preferred_element_type=F32)


def project_kv_kernel(where_ref, *refs):
    sources, (low_ref, up_ref, cos_ref, sin_ref, out_ref, q_ref) = refs[:11], refs[11:17]
    buffers, (scale_ref, wa_ref, wb_ref, semaphores) = refs[17:28], refs[28:]
    inputs = Inputs(sources, buffers, semaphores)
    k = v = 0.0
    for r in range(4):
        k = k + product_a(where_ref, r, inputs.take(1 + r), inputs, scale_ref, wa_ref, 2, 40)
        v = v + product_b(where_ref, r, inputs.take(5 + r), inputs, scale_ref, wb_ref, 2, 40)
    k = k.astype(BF16).astype(F32)
    for h in range(2):
        at = slice(h * 128, (h + 1) * 128)
        out_ref[:, at] = rope(k[:, at], cos_ref[...], sin_ref[...]).astype(BF16)
    v = v.astype(BF16).astype(F32)
    add = jnp.dot(low_ref[:, 64:128], up_ref[...], preferred_element_type=F32)
    out_ref[:, 256:512] = (v + SCALE * add).astype(BF16)
    q_ref[:, :512] = product_a(where_ref, 0, inputs.take(9), inputs, scale_ref, wa_ref, 4, 72)
    q_ref[:, 512:] = product_b(where_ref, 0, inputs.take(10), inputs, scale_ref, wb_ref, 4, 72)


def buffers_of(arrays):
    return [pltpu.VMEM(array.shape, array.dtype) for array in arrays]


def project_kv(where, x, a, b, q_a, q_b, low, up, cosine, sine):
    full = pl.BlockSpec(memory_space=pltpu.VMEM)
    sources = [x, *a, *b, q_a, q_b]
    return pl.pallas_call(
        project_kv_kernel,
        in_specs=[pl.BlockSpec(memory_space=pltpu.SMEM)]
        + [pl.BlockSpec(memory_space=pl.ANY)] * 11
        + [full] * 4,
        out_specs=[full, full],
        out_shape=[
            jax.ShapeDtypeStruct((512, 512), BF16),
            jax.ShapeDtypeStruct((512, 1024), F32),
        ],
        scratch_shapes=buffers_of(sources)
        + [
            pltpu.VMEM((128, 128), F32),
            pltpu.VMEM((1024, 512), BF16),
            pltpu.VMEM((1024, 512), BF16),
            pltpu.SemaphoreType.DMA((11,)),
        ],
        compiler_params=pltpu.CompilerParams(vmem_limit_bytes=VMEM),
        cost_estimate=cost(6e9, 12e6),
        name="project_kv",
    )(where, *sources, low, up, cosine, sine)


LATER = (1, 3, 2)


def project_q_kernel(where_ref, *refs):
    sources, (low_ref, up_ref, cos_ref, sin_ref, out_ref) = refs[:8], refs[8:13]
    buffers, (scale_ref, wa_ref, wb_ref, semaphores) = refs[13:21], refs[21:]
    inputs = Inputs(sources, buffers, semaphores)
    a = b = 0.0
    for n, r in enumerate(LATER):
        a = a + product_a(
            where_ref, r, inputs.take(1 + 2 * n), inputs, scale_ref, wa_ref, 4, 72
        )
        b = b + product_b(
            where_ref, r, inputs.take(2 + 2 * n), inputs, scale_ref, wb_ref, 4, 72
        )
    sum_ref = inputs.take(7)
    a, b = sum_ref[:, :512] + a, sum_ref[:, 512:] + b
    add = jnp.dot(low_ref[:, 0:64], up_ref[...], preferred_element_type=F32)
    for n in range(8):
        at = slice(n % 4 * 128, (n % 4 + 1) * 128)
        q = (a, b)[n // 4][:, at].astype(BF16).astype(F32)
        q = q + SCALE * add[:, n * 128 : (n + 1) * 128]
        out_ref[:, n * 128 : (n + 1) * 128] = rope(q, cos_ref[...], sin_ref[...]).astype(BF16)


def project_q(where, x, a, b, total, low, up, cosine, sine):
    full = pl.BlockSpec(memory_space=pltpu.VMEM)
    sources = [x] + [part[r] for r in LATER for part in (a, b)] + [total]
    return pl.pallas_call(
        project_q_kernel,
        in_specs=[pl.BlockSpec(memory_space=pltpu.SMEM)]
        + [pl.BlockSpec(memory_space=pl.ANY)] * 8
        + [full] * 4,
        out_specs=full,
        out_shape=jax.ShapeDtypeStruct((512, 1024), BF16),
        scratch_shapes=buffers_of(sources)
        + [
            pltpu.VMEM((128, 128), F32),
            pltpu.VMEM((1024, 512), BF16),
            pltpu.VMEM((1024, 512), BF16),
            pltpu.SemaphoreType.DMA((8,)),
        ],
        compiler_params=pltpu.CompilerParams(vmem_limit_bytes=VMEM),
        cost_estimate=cost(6e9, 12e6),
        name="project_q",
    )(where, *sources, low, up, cosine, sine)


def attention_kernel(
    piece_ref,
    q_ref,
    g_ref,
    own_ref,
    other_ref,
    start_ref,
    cos_ref,
    sin_ref,
    out_ref,
    dq_ref,
    dv_own_ref,
    dv_other_ref,
    kv_ref,
    dv_ref,
):
    head, step = pl.program_id(0), pl.program_id(1)

    @pl.when((head == 0) & (step == 0))
    def _():
        for n in range(4):
            at = pl.multiple_of(piece_ref[n] * 128, 128)
            kv_ref[pl.ds(at, 128), :] = own_ref[n * 128 : (n + 1) * 128, :]
            at = pl.multiple_of(piece_ref[4 + n] * 128, 128)
            kv_ref[pl.ds(at, 128), :] = other_ref[n * 128 : (n + 1) * 128, :]

    @pl.when(step == 0)
    def _():
        dv_ref[...] = jnp.zeros_like(dv_ref)

    piece = piece_ref[step]
    first_piece = piece_ref[8 + step]
    first = pl.multiple_of(first_piece * 128, 128)
    q = jnp.concatenate([q_ref[:, i * 128 : (i + 1) * 128] for i in range(4)], axis=0)
    g = jnp.concatenate([g_ref[:, i * 128 : (i + 1) * 128] for i in range(4)], axis=0)
    across = (((1,), (1,)), ((), ()))

    def keys(width):
        at = pl.ds(first, width)
        k = kv_ref[at, pl.ds(pl.multiple_of(head * 128, 128), 128)]
        v = kv_ref[at, pl.ds(pl.multiple_of(256 + head * 128, 128), 128)]
        scores = lax.dot_general(q, k, across, preferred_element_type=F32) * ROOT
        key_at = first + lax.broadcasted_iota(I32, (128, width), 1)
        query_at = piece * 128 + lax.broadcasted_iota(I32, (128, width), 0)
        allowed = (key_at >= start_ref[...]) & (key_at <= query_at)
        bias = jnp.where(allowed, 0.0, -1e30)
        scores = scores + jnp.concatenate([bias] * 4, axis=0)
        top = jnp.max(scores, axis=-1, keepdims=True)
        e = jnp.exp(scores - top)
        p = e * (1.0 / jnp.sum(e, axis=-1, keepdims=True))
        low = p.astype(BF16)
        out = jnp.dot(low, v, preferred_element_type=F32).astype(BF16)
        dp = lax.dot_general(g, v, across, preferred_element_type=F32)
        row = jnp.sum(p * dp, axis=-1, keepdims=True)
        ds = (p * (dp - row) * ROOT).astype(BF16)
        dq = jnp.dot(ds, k, preferred_element_type=F32)
        dv_ref[at, :] += lax.dot_general(
            low, g, (((0,), (0,)), ((), ())), preferred_element_type=F32
        )
        for i in range(4):
            at = slice(i * 128, (i + 1) * 128)
            out_ref[:, at] = out[at]
            dq_ref[:, at] = rope(dq[at], cos_ref[...], -sin_ref[...]).astype(BF16)

    for count in range(1, 6):
        pl.when(piece - first_piece == count - 1)(functools.partial(keys, count * 128))

    @pl.when(step == 3)
    def _():
        for n in range(4):
            at = pl.multiple_of(piece_ref[n] * 128, 128)
            dv_own_ref[n * 128 : (n + 1) * 128, :] = dv_ref[pl.ds(at, 128), :]
            at = pl.multiple_of(piece_ref[4 + n] * 128, 128)
            dv_other_ref[n * 128 : (n + 1) * 128, :] = dv_ref[pl.ds(at, 128), :].astype(BF16)


def attend(pieces, q, g, own, other, starts, cosine, sine):
    block = pl.BlockSpec((128, 512), lambda h, s, p: (s, h))
    whole = pl.BlockSpec((512, 512), lambda h, s, p: (0, 0))
    rows = pl.BlockSpec((128, 128), lambda h, s, p: (s, 0))
    head = pl.BlockSpec((512, 128), lambda h, s, p: (0, h))
    return pl.pallas_call(
        attention_kernel,
        grid_spec=pltpu.PrefetchScalarGridSpec(
            num_scalar_prefetch=1,
            grid=(2, 4),
            in_specs=[
                block,
                block,
                whole,
                whole,
                pl.BlockSpec((128, 1), lambda h, s, p: (s, 0)),
                rows,
                rows,
            ],
            out_specs=[block, block, head, head],
            scratch_shapes=[pltpu.VMEM((1024, 512), BF16), pltpu.VMEM((1024, 128), F32)],
        ),
        out_shape=[
            jax.ShapeDtypeStruct((512, 1024), BF16),
            jax.ShapeDtypeStruct((512, 1024), BF16),
            jax.ShapeDtypeStruct((512, 256), F32),
            jax.ShapeDtypeStruct((512, 256), BF16),
        ],
        compiler_params=pltpu.CompilerParams(vmem_limit_bytes=VMEM),
        name="attention",
    )(pieces, q, g, own, other, starts, cosine, sine)


def place_up_kernel(core_ref, own_ref, other_ref, q_ref, v_ref):
    for ref, core in ((own_ref, core_ref[0]), (other_ref, 1 - core_ref[0])):
        for b in range(10):
            out, at = (q_ref, core * 1024 + b * 128) if b < 8 else (v_ref, core * 256 + b * 128 - 1024)
            out[:, pl.ds(pl.multiple_of(at, 128), 128)] = ref[b * 64 : (b + 1) * 64, :]


def place_up(core, own, other):
    full = pl.BlockSpec(memory_space=pltpu.VMEM)
    return pl.pallas_call(
        place_up_kernel,
        in_specs=[pl.BlockSpec(memory_space=pltpu.SMEM), full, full],
        out_specs=[full, full],
        out_shape=[
            jax.ShapeDtypeStruct((64, 2048), F32),
            jax.ShapeDtypeStruct((64, 512), F32),
        ],
        name="place_up",
    )(core, own, other)


def on_device(hidden, gain, words, scale_zeros, down, query_up, value_up, documents, cotangent):
    f = lax.axis_index("fsdp")
    c = lax.axis_index("ctx")
    x, y, z = f // 16, f // 4 % 4, f % 4
    pair, core = c // 2, c % 2
    where = jnp.stack([x, y, z]).astype(I32)

    with jax.named_scope("pack_words"):
        packed = pack(core[None].astype(I32), words, scale_zeros)
    with jax.named_scope("gather_z"):
        slots = gather_axis(packed, Z)
    with jax.named_scope("gather_inner"):
        part_a, part_b = join_parts(slots)
        part_a, part_b = gather_axis(part_a, Y), gather_axis(part_b, X)
    with jax.named_scope("gather_outer"):
        cuts = ((0, 160), (160, 288))
        kv_a, q_a = join(part_a, cuts, "join_y")
        kv_b, q_b = join(part_b, cuts, "join_x")
        kv_a, kv_b = gather_axis(kv_a, X), gather_axis(kv_b, Y)
        q_a, q_b = gather_axis(q_a, X), gather_axis(q_b, Y)

    with jax.named_scope("norm"):
        wide = hidden[0].astype(F32)
        mean_square = jnp.mean(wide * wide, axis=-1, keepdims=True)
        normed = (wide * lax.rsqrt(mean_square + EPS) * gain.astype(F32)).astype(BF16)
        normed_other = take_from(normed, CORE, 1)
        permuted = permute_features(normed, normed_other)
    with jax.named_scope("adapter_in"):
        low = jnp.concatenate(
            [
                jnp.dot(n, down, preferred_element_type=F32).astype(BF16)
                for n in (normed, normed_other)
            ],
            axis=0,
        )
    up_q = lax.dynamic_slice_in_dim(query_up, core * 1024, 1024, 1)
    up_v = lax.dynamic_slice_in_dim(value_up, core * 256, 256, 1)
    with jax.named_scope("cotangent_heads"):
        g = cotangent[0]
        g_own = lax.dynamic_slice_in_dim(g, core * 1024, 1024, 1)
        g_other = take_from(lax.dynamic_slice_in_dim(g, (1 - core) * 1024, 1024, 1), CORE, 1)
        g = jnp.concatenate([g_own, g_other], axis=0)

    with jax.named_scope("tables"):
        c_pair = (1 - pair) * 2 + core
        pieces = jnp.stack(
            [
                c,
                7 - c,
                c ^ 1,
                7 - (c ^ 1),
                c_pair,
                7 - c_pair,
                c_pair ^ 1,
                7 - (c_pair ^ 1),
            ]
        ).astype(I32)
        at = (pieces[:4, None] * 128 + jnp.arange(128, dtype=I32)[None, :]).reshape(512)
        angles = at.astype(F32)[:, None] * frequencies()[None, :]
        cosine, sine = jnp.cos(angles), jnp.sin(angles)
        cosine = jnp.concatenate([cosine, cosine], axis=1)
        sine = jnp.concatenate([-sine, sine], axis=1)
        docs = documents[0]
        spot = jnp.arange(1024, dtype=I32)
        fresh = jnp.concatenate([jnp.ones((1,), bool), docs[1:] != docs[:-1]])
        start = lax.cummax(jnp.where(fresh, spot, 0))
        start = start.reshape(8, 128)
        starts = jnp.concatenate(
            [lax.dynamic_slice_in_dim(start, pieces[n], 1, 0) for n in range(4)], axis=0
        )
        pieces = jnp.concatenate([pieces, starts[:, 0] // 128])
        starts = starts.reshape(512, 1)

    with jax.named_scope("project_kv"):
        kv, total = project_kv(
            where, permuted, kv_a, kv_b, q_a[0], q_b[0], low, up_v, cosine, sine
        )
        kv_other = take_from(kv, PAIR, 1)
    with jax.named_scope("project_q"):
        q = project_q(where, permuted, q_a, q_b, total, low, up_q, cosine, sine)
    with jax.named_scope("attention"):
        out, dq, dv_own, dv_other = attend(pieces, q, g, kv, kv_other, starts, cosine, sine)
    with jax.named_scope("context_rows"):
        out_other = take_from(out[256:], CORE, 1)
        context = jnp.concatenate([out[:256], out_other, out[:256]], axis=1)
        context = lax.dynamic_slice_in_dim(context, core * 1024, 2048, 1)[None]
    with jax.named_scope("value_grad"):
        dv = (dv_own + take_from(dv_other, PAIR, 1).astype(F32)).astype(BF16)

    rows_dims = (((0,), (0,)), ((), ()))
    across = (((1,), (1,)), ((), ()))
    with jax.named_scope("adapter_grad"):
        term = jnp.concatenate(
            [
                SCALE * lax.dot_general(dq, up_q, across, preferred_element_type=F32),
                SCALE * lax.dot_general(dv, up_v, across, preferred_element_type=F32),
            ],
            axis=1,
        )
        term_other = take_from(term, CORE, 1)
        low_grad = (term + jnp.concatenate([term_other[256:], term_other[:256]], axis=0)).astype(BF16)
    with jax.named_scope("up_terms"):
        up = jnp.concatenate(
            [
                SCALE * lax.dot_general(low[:, :64], dq, rows_dims, preferred_element_type=F32),
                SCALE * lax.dot_general(low[:, 64:], dv, rows_dims, preferred_element_type=F32),
            ],
            axis=1,
        )
        up = jnp.concatenate([up[:, b * 128 : (b + 1) * 128] for b in range(10)], axis=0)
    with jax.named_scope("down_terms"):
        grad = lax.dot_general(
            normed, low_grad[:256], rows_dims, preferred_element_type=F32
        ) + lax.dot_general(normed_other, low_grad[256:], rows_dims, preferred_element_type=F32)
        grad = lax.dynamic_index_in_dim(grad.reshape(128, 2, 16, 128), core, 1, keepdims=False)
    with jax.named_scope("sum_plane"):
        parts = jnp.concatenate([grad.reshape(16, 128, 128), up.reshape(16, 40, 128)], axis=1)
        total = jnp.sum(exchange(parts.astype(BF16), PLANE, "fsdp").astype(F32), axis=0)
    with jax.named_scope("sum_z"):
        parts = jnp.concatenate(
            [total[:128].reshape(8, 16, 128), jnp.broadcast_to(total[None, 128:], (8, 40, 128))],
            axis=1,
        )
        total = jnp.sum(exchange(parts, COLUMN, AXES), axis=0)
        grad_down = total[:16]
    with jax.named_scope("share_up"):
        up = exchange(jnp.broadcast_to(total[None, 16:], (16, 40, 128)), PLANE, "fsdp")
        up = up.reshape(640, 128)
        query_up_gradient, value_up_gradient = place_up(
            core[None].astype(I32), up, take_from(up, CORE, 1)
        )
    return context, grad_down, query_up_gradient, value_up_gradient


def solution(mesh):
    return jax.shard_map(
        on_device,
        mesh=mesh,
        in_specs=(
            P("fsdp", "ctx", None),
            P(),
            P("fsdp", None, None),
            P("fsdp", None, None),
            P(),
            P(),
            P(),
            P("fsdp", None),
            P("fsdp", "ctx", None),
        ),
        out_specs=(P("fsdp", "ctx", None), P(("fsdp", "ctx"), None), P(), P()),
        check_vma=False,
    )
```

```python
import functools
import math

import jax
import jax.numpy as jnp
import numpy as np
from jax import lax
from jax.experimental import pallas as pl
from jax.experimental.pallas import tpu as pltpu
from jax.sharding import PartitionSpec as P

HEAD = 128
SCALE = 0.25
EPS = 1e-05
THETA = 500000.0
ROOT = 1.0 / math.sqrt(HEAD)
LOG2E = math.log2(math.e)
AXES = ("fsdp", "ctx")
VMEM = 32 * 1024 * 1024
F32, BF16, I32 = jnp.float32, jnp.bfloat16, jnp.int32


def place(l):
    f, c = divmod(l, 4)
    return [f // 16, f // 4 % 4, f % 4, c // 2, c % 2]


def index(p):
    return ((p[0] * 4 + p[1]) * 4 + p[2]) * 4 + p[3] * 2 + p[4]


SIZES = (4, 4, 4, 2, 2)
X, Y, Z, PAIR, CORE = range(5)


def take_from(value, axis, step):
    pairs = []
    for l in range(256):
        p = place(l)
        p[axis] = (p[axis] - step) % SIZES[axis]
        pairs.append((l, index(p)))
    return lax.ppermute(value, AXES, pairs)


def gather_axis(value, axis):
    return [value] + [take_from(value, axis, r) for r in (1, 2, 3)]


PLANE = [[4 * n + z for n in range(16)] for z in range(4)]
COLUMN = [
    [index((x, y, z, pair, core)) for z in range(4) for pair in range(2)]
    for x in range(4)
    for y in range(4)
    for core in range(2)
]


def exchange(parts, groups, axes):
    return lax.all_to_all(parts, axes, 0, 0, tiled=True, axis_index_groups=groups)


def frequencies():
    exponent = jnp.arange(0, HEAD, 2, dtype=F32) / HEAD
    inverse = 1.0 / THETA**exponent
    wavelength = 2.0 * math.pi / inverse
    blend = (8192.0 / wavelength - 1.0) / 3.0
    middle = (1.0 - blend) * inverse / 8.0 + blend * inverse
    return jnp.where(
        wavelength < 2048.0, inverse, jnp.where(wavelength > 8192.0, inverse / 8.0, middle)
    )


def scale_code(scale):
    m = scale.astype(F32) * 16.0
    e = jnp.full(m.shape, 4, I32)
    for k in (64, 64, 32, 16, 8, 4, 2, 1):
        small = m < 2.0 ** (8 - k)
        m = jnp.where(small, m * 2.0**k, m)
        e = jnp.where(small, e + k, e)
    return m.astype(I32) + 256 * e


def decode_scale(code):
    s = jnp.bitwise_and(code, 255).astype(F32)
    e = jnp.right_shift(code, 8)
    for k in (1, 2, 4, 8, 16, 32, 64):
        s = jnp.where(jnp.bitwise_and(e, k) != 0, s * 2.0**-k, s)
    return jnp.where(jnp.bitwise_and(e, 128) != 0, (s * 2.0**-64) * 2.0**-64, s)


def cost(flops, moved):
    return pl.CostEstimate(flops=int(flops), bytes_accessed=int(moved), transcendentals=0)


def pack_kernel(core_ref, words_ref, params_ref, out_ref):
    core = core_ref[0]
    row = 0
    for first, step, blocks, pad in (
        (2048, 256, 2, 4),
        (0, 1024, 4, 0),
        (2560, 256, 2, 4),
        (512, 1024, 4, 0),
    ):
        for b in range(blocks):
            at = pl.ds(pl.multiple_of(first + core * step + b * 128, 128), 128)
            out_ref[row + 16 * b : row + 16 * b + 16, :] = words_ref[0, :, at]
            params = params_ref[0, :, at].astype(F32)
            tail = row + 16 * blocks + b
            out_ref[tail : tail + 1, :] = scale_code(params[0:1])
            out_ref[tail + blocks : tail + blocks + 1, :] = (params[1:2] * 128.0).astype(I32)
        row += 18 * blocks
        if pad:
            out_ref[row : row + pad, :] = jnp.zeros((pad, 128), I32)
            row += pad


def pack(core, words, params):
    full = pl.BlockSpec(memory_space=pltpu.VMEM)
    return pl.pallas_call(
        pack_kernel,
        in_specs=[pl.BlockSpec(memory_space=pltpu.SMEM), full, full],
        out_specs=full,
        out_shape=jax.ShapeDtypeStruct((224, 128), I32),
        name="pack_words",
    )(core, words, params)


def permute_kernel(own_ref, other_ref, p_ref, out_ref):
    p = p_ref[...]
    for n in range(4):
        at = slice(n * 256, (n + 1) * 256)
        out_ref[:256, at] = jnp.dot(own_ref[:, at], p, preferred_element_type=F32).astype(BF16)
        out_ref[256:, at] = jnp.dot(other_ref[:, at], p, preferred_element_type=F32).astype(BF16)


def permute_features(own, other):
    d = np.arange(256)
    source = (d // 64) * 64 + 4 * (d % 16) + (d % 64) // 16
    p = np.zeros((256, 256), np.float32)
    p[source, d] = 1.0
    return pl.pallas_call(
        permute_kernel,
        grid=(4,),
        in_specs=[
            pl.BlockSpec((256, 1024), lambda i: (0, i)),
            pl.BlockSpec((256, 1024), lambda i: (0, i)),
            pl.BlockSpec((256, 256), lambda i: (0, 0)),
        ],
        out_specs=pl.BlockSpec((512, 1024), lambda i: (0, i)),
        cost_estimate=cost(1.1e9, 8.4e6),
        out_shape=jax.ShapeDtypeStruct((512, 4096), BF16),
        name="permute_features",
    )(own, other, jnp.asarray(p, BF16))


def join_kernel(moves, count, *refs):
    ins, outs, semaphores = refs[:4], refs[4 : 4 + count], refs[4 + count]
    copies = []
    for n, (source, first, target, at, rows) in enumerate(moves):
        copies.append(
            pltpu.make_async_copy(
                ins[source].at[pl.ds(first, rows), :],
                outs[target].at[pl.ds(at, rows), :],
                semaphores.at[n],
            )
        )
        copies[-1].start()
    for copy in copies:
        copy.wait()


def join(parts, moves, sizes, name):
    anywhere = pl.BlockSpec(memory_space=pl.ANY)
    return pl.pallas_call(
        functools.partial(join_kernel, moves, len(sizes)),
        in_specs=[anywhere] * 4,
        out_specs=[anywhere] * len(sizes),
        out_shape=[jax.ShapeDtypeStruct((n, 128), I32) for n in sizes],
        scratch_shapes=[pltpu.SemaphoreType.DMA((len(moves),))],
        compiler_params=pltpu.CompilerParams(vmem_limit_bytes=1024 * 1024),
        cost_estimate=cost(0, 4e6),
        name=name,
    )(*parts)


def join_slots(slots):
    moves = []
    for half in range(2):
        for n in range(4):
            moves.append((n, half * 112, half, n * 40, 40))
            moves.append((n, half * 112 + 40, half, 160 + n * 72, 72))
    return join(slots, moves, (448, 448), "join_z")


def join_inner(parts, name):
    moves = []
    for n in range(4):
        moves.append((n, 0, 0, n * 160, 160))
        moves.append((n, 160, 1, n * 288, 288))
    return join(parts, moves, (640, 1152), name)


def dequantize(where_ref, ref, scale_ref, w_ref, first, outer_axis, r, blocks, rows):
    last = 16 * blocks
    pad = rows - last
    codes = jnp.concatenate([ref[n * rows + last : (n + 1) * rows, :] for n in range(16)], axis=0)
    row_kind = jnp.bitwise_and(lax.broadcasted_iota(I32, codes.shape, 0), pad - 1)
    scale_ref[...] = jnp.where(
        row_kind < blocks, decode_scale(codes), codes.astype(F32) * (1.0 / 128.0)
    )
    outer = (where_ref[outer_axis] + r) % 4
    outer_step, inner_step = (1024, 256) if outer_axis == X else (256, 1024)
    inner = where_ref[Y if outer_axis == X else X]

    def one(n, carry):
        inner_at = (inner + n // 4) % 4
        slot_at = (where_ref[Z] + n % 4) % 4
        row = pl.multiple_of(outer * outer_step + inner_at * inner_step + slot_at * 64, 64)
        base = pl.multiple_of(n * rows, 8)
        tail = scale_ref[pl.ds(pl.multiple_of(n * pad, 8), pad), :]
        for b in range(blocks):
            words = ref[pl.ds(base + 16 * b, 16), :]
            scale = jnp.broadcast_to(tail[b : b + 1], (16, 128))
            zero = jnp.broadcast_to(tail[blocks + b : blocks + b + 1], (16, 128))
            at = slice(first + b * 128, first + (b + 1) * 128)
            for i in range(4):
                code = jnp.bitwise_and(jnp.right_shift(words, 4 * i), 15).astype(F32)
                w_ref[pl.ds(row + 16 * i, 16), at] = ((code - zero) * scale).astype(BF16)
        return carry

    lax.fori_loop(0, 16, one, 0, unroll=4)


def rope(x, cosine, sine):
    return x * cosine + pltpu.roll(x, 64, 1) * sine


class Inputs:
    def __init__(self, sources, buffers, semaphores, order):
        self.buffers, self.order = buffers, order
        self.copies = [
            pltpu.make_async_copy(source, buffers[n], semaphores.at[n])
            for n, source in enumerate(sources)
        ]
        for n in order:
            self.copies[n].start()

    def take(self, n):
        self.copies[n].wait()
        return self.buffers[n]


ORDER = (0, 1, 2, 3, 4, 8, 5, 6, 7)


def project_kv_kernel(where_ref, *refs):
    sources, (low_ref, up_ref, cos_ref, sin_ref, out_ref) = refs[:9], refs[9:14]
    buffers, (scale_ref, w_ref, semaphores) = refs[14:23], refs[23:]
    inputs = Inputs(sources, buffers, semaphores, ORDER)
    for r in range(4):
        dequantize(where_ref, inputs.take(r), scale_ref, w_ref, 0, X, r, 2, 40)
    for r in range(4):
        dequantize(where_ref, inputs.take(4 + r), scale_ref, w_ref, 256, Y, r, 2, 40)
    x_ref = inputs.take(8)
    k = jnp.dot(x_ref[...], w_ref[:, :256], preferred_element_type=F32).astype(BF16).astype(F32)
    for h in range(2):
        at = slice(h * 128, (h + 1) * 128)
        out_ref[:, at] = rope(k[:, at], cos_ref[...], sin_ref[...]).astype(BF16)
    v = jnp.dot(x_ref[...], w_ref[:, 256:], preferred_element_type=F32).astype(BF16).astype(F32)
    add = jnp.dot(low_ref[:, 64:128], up_ref[...], preferred_element_type=F32)
    out_ref[:, 256:512] = (v + SCALE * add).astype(BF16)


def project_q_kernel(where_ref, *refs):
    sources, (low_ref, up_ref, cos_ref, sin_ref, out_ref) = refs[:9], refs[9:14]
    buffers, (scale_ref, w_ref, semaphores) = refs[14:23], refs[23:]
    inputs = Inputs(sources, buffers, semaphores, ORDER)
    for r in range(4):
        dequantize(where_ref, inputs.take(r), scale_ref, w_ref, 0, X, r, 4, 72)
    for r in range(4):
        dequantize(where_ref, inputs.take(4 + r), scale_ref, w_ref, 512, Y, r, 4, 72)
    x_ref = inputs.take(8)
    for t in range(4):
        at = slice(t * 256, (t + 1) * 256)
        q = jnp.dot(x_ref[...], w_ref[:, at], preferred_element_type=F32).astype(BF16).astype(F32)
        add = jnp.dot(low_ref[:, 0:64], up_ref[:, at], preferred_element_type=F32)
        q = q + SCALE * add
        for h in range(2):
            at = slice(t * 256 + h * 128, t * 256 + (h + 1) * 128)
            out_ref[:, at] = rope(
                q[:, h * 128 : (h + 1) * 128], cos_ref[...], sin_ref[...]
            ).astype(BF16)


def project(kernel, columns, where, x, a, b, low, up, cosine, sine, name):
    full = pl.BlockSpec(memory_space=pltpu.VMEM)
    sources = [*a, *b, x]
    return pl.pallas_call(
        kernel,
        in_specs=[pl.BlockSpec(memory_space=pltpu.SMEM)]
        + [pl.BlockSpec(memory_space=pl.ANY)] * 9
        + [full] * 4,
        out_specs=full,
        out_shape=jax.ShapeDtypeStruct((512, columns), BF16),
        scratch_shapes=[pltpu.VMEM(array.shape, array.dtype) for array in sources]
        + [
            pltpu.VMEM((128, 128), F32),
            pltpu.VMEM((4096, columns), BF16),
            pltpu.SemaphoreType.DMA((9,)),
        ],
        compiler_params=pltpu.CompilerParams(vmem_limit_bytes=VMEM),
        cost_estimate=cost(6e9, 12e6),
        name=name,
    )(where, *sources, low, up, cosine, sine)


def project_kv(where, x, a, b, low, up, cosine, sine):
    return project(project_kv_kernel, 512, where, x, a, b, low, up, cosine, sine, "project_kv")


def project_q(where, x, a, b, low, up, cosine, sine):
    return project(project_q_kernel, 1024, where, x, a, b, low, up, cosine, sine, "project_q")


def attention_kernel(
    piece_ref,
    q_ref,
    g_ref,
    own_ref,
    other_ref,
    start_ref,
    cos_ref,
    sin_ref,
    out_ref,
    dq_ref,
    dv_own_ref,
    dv_other_ref,
    kv_ref,
    dv_ref,
):
    head, step = pl.program_id(0), pl.program_id(1)

    @pl.when((head == 0) & (step == 0))
    def _():
        for n in range(4):
            at = pl.multiple_of(piece_ref[n] * 128, 128)
            kv_ref[pl.ds(at, 128), :] = own_ref[n * 128 : (n + 1) * 128, :]
            at = pl.multiple_of(piece_ref[4 + n] * 128, 128)
            kv_ref[pl.ds(at, 128), :] = other_ref[n * 128 : (n + 1) * 128, :]

    @pl.when(step == 0)
    def _():
        dv_ref[...] = jnp.zeros_like(dv_ref)

    piece = piece_ref[step]
    first_piece = piece_ref[8 + step]
    first = pl.multiple_of(first_piece * 128, 128)
    q = jnp.concatenate([q_ref[:, i * 128 : (i + 1) * 128] for i in range(4)], axis=0)
    g = jnp.concatenate([g_ref[:, i * 128 : (i + 1) * 128] for i in range(4)], axis=0)
    across = (((1,), (1,)), ((), ()))

    def keys(width):
        at = pl.ds(first, width)
        k = kv_ref[at, pl.ds(pl.multiple_of(head * 128, 128), 128)]
        v = kv_ref[at, pl.ds(pl.multiple_of(256 + head * 128, 128), 128)]
        key_at = first + lax.broadcasted_iota(I32, (128, width), 1)
        query_at = piece * 128 + lax.broadcasted_iota(I32, (128, width), 0)
        allowed = (key_at >= start_ref[...]) & (key_at <= query_at)
        bias = jnp.where(allowed, 0.0, -1e30)
        bias = jnp.concatenate([bias] * 4, axis=0)
        lows = []
        for n in range(1):
            some = slice(n * 512, (n + 1) * 512)
            scores = lax.dot_general(q[some], k, across, preferred_element_type=F32)
            scores = scores * (ROOT * LOG2E) + bias
            dp = lax.dot_general(g[some], v, across, preferred_element_type=F32)
            top = jnp.max(scores, axis=-1, keepdims=True)
            e = jnp.exp2(scores - top)
            p = e * (1.0 / jnp.sum(e, axis=-1, keepdims=True))
            low = p.astype(BF16)
            lows.append(low)
            out = jnp.dot(low, v, preferred_element_type=F32).astype(BF16)
            row = jnp.sum(p * dp, axis=-1, keepdims=True)
            ds = ((p * ROOT) * (dp - row)).astype(BF16)
            dq = jnp.dot(ds, k, preferred_element_type=F32)
            for i in range(4):
                to = slice((n * 4 + i) * 128, (n * 4 + i + 1) * 128)
                rows = slice(i * 128, (i + 1) * 128)
                out_ref[:, to] = out[rows]
                dq_ref[:, to] = rope(dq[rows], cos_ref[...], -sin_ref[...]).astype(BF16)
        dv_ref[at, :] += lax.dot_general(
            jnp.concatenate(lows, axis=0), g, (((0,), (0,)), ((), ())), preferred_element_type=F32
        )

    for count in range(1, 6):
        pl.when(piece - first_piece == count - 1)(functools.partial(keys, count * 128))

    @pl.when(step == 3)
    def _():
        for n in range(4):
            at = pl.multiple_of(piece_ref[n] * 128, 128)
            dv_own_ref[n * 128 : (n + 1) * 128, :] = dv_ref[pl.ds(at, 128), :]
            at = pl.multiple_of(piece_ref[4 + n] * 128, 128)
            dv_other_ref[n * 128 : (n + 1) * 128, :] = dv_ref[pl.ds(at, 128), :].astype(BF16)


def attend(pieces, q, g, own, other, starts, cosine, sine):
    block = pl.BlockSpec((128, 512), lambda h, s, p: (s, h))
    whole = pl.BlockSpec((512, 512), lambda h, s, p: (0, 0))
    rows = pl.BlockSpec((128, 128), lambda h, s, p: (s, 0))
    head = pl.BlockSpec((512, 128), lambda h, s, p: (0, h))
    return pl.pallas_call(
        attention_kernel,
        grid_spec=pltpu.PrefetchScalarGridSpec(
            num_scalar_prefetch=1,
            grid=(2, 4),
            in_specs=[
                block,
                block,
                whole,
                whole,
                pl.BlockSpec((128, 1), lambda h, s, p: (s, 0)),
                rows,
                rows,
            ],
            out_specs=[block, block, head, head],
            scratch_shapes=[pltpu.VMEM((1024, 512), BF16), pltpu.VMEM((1024, 128), F32)],
        ),
        out_shape=[
            jax.ShapeDtypeStruct((512, 1024), BF16),
            jax.ShapeDtypeStruct((512, 1024), BF16),
            jax.ShapeDtypeStruct((512, 256), F32),
            jax.ShapeDtypeStruct((512, 256), BF16),
        ],
        compiler_params=pltpu.CompilerParams(vmem_limit_bytes=VMEM),
        name="attention",
    )(pieces, q, g, own, other, starts, cosine, sine)


def place_up_kernel(core_ref, own_ref, other_ref, q_ref, v_ref):
    for ref, core in ((own_ref, core_ref[0]), (other_ref, 1 - core_ref[0])):
        for b in range(10):
            out, at = (q_ref, core * 1024 + b * 128) if b < 8 else (v_ref, core * 256 + b * 128 - 1024)
            out[:, pl.ds(pl.multiple_of(at, 128), 128)] = ref[b * 64 : (b + 1) * 64, :]


def place_up(core, own, other):
    full = pl.BlockSpec(memory_space=pltpu.VMEM)
    return pl.pallas_call(
        place_up_kernel,
        in_specs=[pl.BlockSpec(memory_space=pltpu.SMEM), full, full],
        out_specs=[full, full],
        out_shape=[
            jax.ShapeDtypeStruct((64, 2048), F32),
            jax.ShapeDtypeStruct((64, 512), F32),
        ],
        name="place_up",
    )(core, own, other)


def on_device(hidden, gain, words, scale_zeros, down, query_up, value_up, documents, cotangent):
    f = lax.axis_index("fsdp")
    c = lax.axis_index("ctx")
    x, y, z = f // 16, f // 4 % 4, f % 4
    pair, core = c // 2, c % 2
    where = jnp.stack([x, y, z]).astype(I32)

    with jax.named_scope("pack_words"):
        packed = pack(core[None].astype(I32), words, scale_zeros)
    with jax.named_scope("gather_z"):
        slots = gather_axis(packed, Z)
    with jax.named_scope("norm"):
        wide = hidden[0].astype(F32)
        mean_square = jnp.mean(wide * wide, axis=-1, keepdims=True)
        normed = (wide * lax.rsqrt(mean_square + EPS) * gain.astype(F32)).astype(BF16)
        normed_other = take_from(normed, CORE, 1)
    with jax.named_scope("gather_inner"):
        *slots, normed_other = lax.optimization_barrier((*slots, normed_other))
        part_a, part_b = join_slots(slots)
        part_a, part_b = gather_axis(part_a, Y), gather_axis(part_b, X)
    with jax.named_scope("permute_features"):
        permuted = permute_features(normed, normed_other)
        part_a, part_b, permuted = lax.optimization_barrier((part_a, part_b, permuted))
    with jax.named_scope("gather_outer"):
        kv_a, q_a = join_inner(part_a, "join_y")
        kv_b, q_b = join_inner(part_b, "join_x")
        kv_a, q_a, kv_b, q_b = lax.optimization_barrier((kv_a, q_a, kv_b, q_b))
        kv_a, kv_b = gather_axis(kv_a, X), gather_axis(kv_b, Y)
        q_a, q_b = gather_axis(q_a, X), gather_axis(q_b, Y)
        q_a[1], q_b[1], cotangent = lax.optimization_barrier((q_a[1], q_b[1], cotangent))

    with jax.named_scope("adapter_in"):
        low = jnp.concatenate(
            [
                jnp.dot(n, down, preferred_element_type=F32).astype(BF16)
                for n in (normed, normed_other)
            ],
            axis=0,
        )
    up_q = lax.dynamic_slice_in_dim(query_up, core * 1024, 1024, 1)
    up_v = lax.dynamic_slice_in_dim(value_up, core * 256, 256, 1)
    with jax.named_scope("cotangent_heads"):
        g = cotangent[0]
        g_own = lax.dynamic_slice_in_dim(g, core * 1024, 1024, 1)
        g_other = take_from(lax.dynamic_slice_in_dim(g, (1 - core) * 1024, 1024, 1), CORE, 1)
        g = jnp.concatenate([g_own, g_other], axis=0)

    with jax.named_scope("tables"):
        c_pair = (1 - pair) * 2 + core
        pieces = jnp.stack(
            [
                c,
                7 - c,
                c ^ 1,
                7 - (c ^ 1),
                c_pair,
                7 - c_pair,
                c_pair ^ 1,
                7 - (c_pair ^ 1),
            ]
        ).astype(I32)
        at = (pieces[:4, None] * 128 + jnp.arange(128, dtype=I32)[None, :]).reshape(512)
        angles = at.astype(F32)[:, None] * frequencies()[None, :]
        cosine, sine = jnp.cos(angles), jnp.sin(angles)
        cosine = jnp.concatenate([cosine, cosine], axis=1)
        sine = jnp.concatenate([-sine, sine], axis=1)
        docs = documents[0]
        spot = jnp.arange(1024, dtype=I32)
        fresh = jnp.concatenate([jnp.ones((1,), bool), docs[1:] != docs[:-1]])
        start = lax.cummax(jnp.where(fresh, spot, 0))
        start = start.reshape(8, 128)
        starts = jnp.concatenate(
            [lax.dynamic_slice_in_dim(start, pieces[n], 1, 0) for n in range(4)], axis=0
        )
        pieces = jnp.concatenate([pieces, starts[:, 0] // 128])
        starts = starts.reshape(512, 1)

    with jax.named_scope("project_kv"):
        kv = project_kv(where, permuted, kv_a, kv_b, low, up_v, cosine, sine)
        kv_other = take_from(kv, PAIR, 1)
    with jax.named_scope("project_q"):
        q = project_q(where, permuted, q_a, q_b, low, up_q, cosine, sine)
    with jax.named_scope("attention"):
        out, dq, dv_own, dv_other = attend(pieces, q, g, kv, kv_other, starts, cosine, sine)
    with jax.named_scope("context_rows"):
        out_other = take_from(out[256:], CORE, 1)
        context = jnp.concatenate([out[:256], out_other, out[:256]], axis=1)
        context = lax.dynamic_slice_in_dim(context, core * 1024, 2048, 1)[None]
    with jax.named_scope("value_grad"):
        dv = (dv_own + take_from(dv_other, PAIR, 1).astype(F32)).astype(BF16)

    rows_dims = (((0,), (0,)), ((), ()))
    across = (((1,), (1,)), ((), ()))
    with jax.named_scope("adapter_grad"):
        term = jnp.concatenate(
            [
                SCALE * lax.dot_general(dq, up_q, across, preferred_element_type=F32),
                SCALE * lax.dot_general(dv, up_v, across, preferred_element_type=F32),
            ],
            axis=1,
        )
        term_other = take_from(term, CORE, 1)
        low_grad = (term + jnp.concatenate([term_other[256:], term_other[:256]], axis=0)).astype(BF16)
    with jax.named_scope("up_terms"):
        up = jnp.concatenate(
            [
                SCALE * lax.dot_general(low[:, :64], dq, rows_dims, preferred_element_type=F32),
                SCALE * lax.dot_general(low[:, 64:], dv, rows_dims, preferred_element_type=F32),
            ],
            axis=1,
        )
        up = jnp.concatenate([up[:, b * 128 : (b + 1) * 128] for b in range(10)], axis=0)
    with jax.named_scope("down_terms"):
        grad = lax.dot_general(
            normed, low_grad[:256], rows_dims, preferred_element_type=F32
        ) + lax.dot_general(normed_other, low_grad[256:], rows_dims, preferred_element_type=F32)
        grad = lax.dynamic_index_in_dim(grad.reshape(128, 2, 16, 128), core, 1, keepdims=False)
    with jax.named_scope("sum_plane"):
        parts = jnp.concatenate([grad.reshape(16, 128, 128), up.reshape(16, 40, 128)], axis=1)
        total = jnp.sum(exchange(parts.astype(BF16), PLANE, "fsdp").astype(F32), axis=0)
    with jax.named_scope("sum_z"):
        parts = jnp.concatenate(
            [total[:128].reshape(8, 16, 128), jnp.broadcast_to(total[None, 128:], (8, 40, 128))],
            axis=1,
        )
        total = jnp.sum(exchange(parts, COLUMN, AXES), axis=0)
        grad_down = total[:16]
    with jax.named_scope("share_up"):
        up = exchange(jnp.broadcast_to(total[None, 16:], (16, 40, 128)), PLANE, "fsdp")
        up = up.reshape(640, 128)
        query_up_gradient, value_up_gradient = place_up(
            core[None].astype(I32), up, take_from(up, CORE, 1)
        )
    return context, grad_down, query_up_gradient, value_up_gradient


def solution(mesh):
    return jax.shard_map(
        on_device,
        mesh=mesh,
        in_specs=(
            P("fsdp", "ctx", None),
            P(),
            P("fsdp", None, None),
            P("fsdp", None, None),
            P(),
            P(),
            P(),
            P("fsdp", None),
            P("fsdp", "ctx", None),
        ),
        out_specs=(P("fsdp", "ctx", None), P(("fsdp", "ctx"), None), P(), P()),
        check_vma=False,
    )
```

```python
import functools
import math

import jax
import jax.numpy as jnp
import numpy as np
from jax import lax
from jax.experimental import pallas as pl
from jax.experimental.pallas import tpu as pltpu
from jax.sharding import PartitionSpec as P

HEAD = 128
SCALE = 0.25
EPS = 1e-05
THETA = 500000.0
ROOT = 1.0 / math.sqrt(HEAD)
LOG2E = math.log2(math.e)
AXES = ("fsdp", "ctx")
VMEM = 32 * 1024 * 1024
F32, BF16, I32 = jnp.float32, jnp.bfloat16, jnp.int32


def place(l):
    f, c = divmod(l, 4)
    return [f // 16, f // 4 % 4, f % 4, c // 2, c % 2]


def index(p):
    return ((p[0] * 4 + p[1]) * 4 + p[2]) * 4 + p[3] * 2 + p[4]


SIZES = (4, 4, 4, 2, 2)
X, Y, Z, PAIR, CORE = range(5)


def take_from(value, axis, step):
    pairs = []
    for l in range(256):
        p = place(l)
        p[axis] = (p[axis] - step) % SIZES[axis]
        pairs.append((l, index(p)))
    return lax.ppermute(value, AXES, pairs)


def gather_axis(value, axis):
    return [value] + [take_from(value, axis, r) for r in (1, 2, 3)]


PLANE = [[4 * n + z for n in range(16)] for z in range(4)]
COLUMN = [
    [index((x, y, z, pair, core)) for z in range(4) for pair in range(2)]
    for x in range(4)
    for y in range(4)
    for core in range(2)
]


def exchange(parts, groups, axes):
    return lax.all_to_all(parts, axes, 0, 0, tiled=True, axis_index_groups=groups)


def frequencies():
    exponent = jnp.arange(0, HEAD, 2, dtype=F32) / HEAD
    inverse = 1.0 / THETA**exponent
    wavelength = 2.0 * math.pi / inverse
    blend = (8192.0 / wavelength - 1.0) / 3.0
    middle = (1.0 - blend) * inverse / 8.0 + blend * inverse
    return jnp.where(
        wavelength < 2048.0, inverse, jnp.where(wavelength > 8192.0, inverse / 8.0, middle)
    )


def scale_code(scale):
    m = scale.astype(F32) * 16.0
    e = jnp.full(m.shape, 4, I32)
    for k in (64, 64, 32, 16, 8, 4, 2, 1):
        small = m < 2.0 ** (8 - k)
        m = jnp.where(small, m * 2.0**k, m)
        e = jnp.where(small, e + k, e)
    return m.astype(I32) + 256 * e


def decode_scale(code):
    s = jnp.bitwise_and(code, 255).astype(F32)
    e = jnp.right_shift(code, 8)
    for k in (1, 2, 4, 8, 16, 32, 64):
        s = jnp.where(jnp.bitwise_and(e, k) != 0, s * 2.0**-k, s)
    return jnp.where(jnp.bitwise_and(e, 128) != 0, (s * 2.0**-64) * 2.0**-64, s)


def cost(flops, moved):
    return pl.CostEstimate(flops=int(flops), bytes_accessed=int(moved), transcendentals=0)


def pack_kernel(core_ref, words_ref, params_ref, out_ref):
    core = core_ref[0]
    row = 0
    for first, step, blocks, pad in (
        (2048, 256, 2, 4),
        (0, 1024, 4, 0),
        (2560, 256, 2, 4),
        (512, 1024, 4, 0),
    ):
        for b in range(blocks):
            at = pl.ds(pl.multiple_of(first + core * step + b * 128, 128), 128)
            out_ref[row + 16 * b : row + 16 * b + 16, :] = words_ref[0, :, at]
            params = params_ref[0, :, at].astype(F32)
            tail = row + 16 * blocks + b
            out_ref[tail : tail + 1, :] = scale_code(params[0:1])
            out_ref[tail + blocks : tail + blocks + 1, :] = (params[1:2] * 128.0).astype(I32)
        row += 18 * blocks
        if pad:
            out_ref[row : row + pad, :] = jnp.zeros((pad, 128), I32)
            row += pad


def pack(core, words, params):
    full = pl.BlockSpec(memory_space=pltpu.VMEM)
    return pl.pallas_call(
        pack_kernel,
        in_specs=[pl.BlockSpec(memory_space=pltpu.SMEM), full, full],
        out_specs=full,
        out_shape=jax.ShapeDtypeStruct((224, 128), I32),
        name="pack_words",
    )(core, words, params)


def permute_kernel(own_ref, other_ref, p_ref, half_ref, out_ref, some_ref):
    p, half = p_ref[...], half_ref[...]
    for rows, ref in ((slice(0, 256), own_ref), (slice(256, 512), other_ref)):
        for n in range(4):
            x = ref[:, n * 256 : (n + 1) * 256]
            out_ref[rows, n * 256 : (n + 1) * 256] = jnp.dot(
                x, p, preferred_element_type=F32
            ).astype(BF16)
            some_ref[rows, n * 128 : (n + 1) * 128] = jnp.dot(
                x, half, preferred_element_type=F32
            ).astype(BF16)


def permute_features(own, other, core):
    d = np.arange(256)
    source = (d // 64) * 64 + 4 * (d % 16) + (d % 64) // 16
    p = np.zeros((256, 256), np.float32)
    p[source, d] = 1.0
    d = np.arange(128)
    half = np.zeros((2, 256, 128), np.float32)
    for n in range(2):
        half[n, (d // 16) * 32 + n * 16 + d % 16, d] = 1.0
    half = lax.dynamic_index_in_dim(jnp.asarray(half, BF16), core, 0, keepdims=False)
    return pl.pallas_call(
        permute_kernel,
        grid=(4,),
        in_specs=[
            pl.BlockSpec((256, 1024), lambda i: (0, i)),
            pl.BlockSpec((256, 1024), lambda i: (0, i)),
            pl.BlockSpec((256, 256), lambda i: (0, 0)),
            pl.BlockSpec((256, 128), lambda i: (0, 0)),
        ],
        out_specs=[
            pl.BlockSpec((512, 1024), lambda i: (0, i)),
            pl.BlockSpec((512, 512), lambda i: (0, i)),
        ],
        cost_estimate=cost(1.6e9, 1.0e7),
        out_shape=[
            jax.ShapeDtypeStruct((512, 4096), BF16),
            jax.ShapeDtypeStruct((512, 2048), BF16),
        ],
        name="permute_features",
    )(own, other, jnp.asarray(p, BF16), half)


def join_kernel(moves, count, *refs):
    ins, outs, semaphores = refs[:4], refs[4 : 4 + count], refs[4 + count]
    copies = []
    for n, (source, first, target, at, rows) in enumerate(moves):
        copies.append(
            pltpu.make_async_copy(
                ins[source].at[pl.ds(first, rows), :],
                outs[target].at[pl.ds(at, rows), :],
                semaphores.at[n],
            )
        )
        copies[-1].start()
    for copy in copies:
        copy.wait()


def join(parts, moves, sizes, name):
    anywhere = pl.BlockSpec(memory_space=pl.ANY)
    return pl.pallas_call(
        functools.partial(join_kernel, moves, len(sizes)),
        in_specs=[anywhere] * 4,
        out_specs=[anywhere] * len(sizes),
        out_shape=[jax.ShapeDtypeStruct((n, 128), I32) for n in sizes],
        scratch_shapes=[pltpu.SemaphoreType.DMA((len(moves),))],
        compiler_params=pltpu.CompilerParams(vmem_limit_bytes=1024 * 1024),
        cost_estimate=cost(0, 4e6),
        name=name,
    )(*parts)


def join_slots(slots):
    moves = []
    for half in range(2):
        for n in range(4):
            moves.append((n, half * 112, half, n * 40, 40))
            moves.append((n, half * 112 + 40, half, 160 + n * 72, 72))
    return join(slots, moves, (448, 448), "join_z")


def join_inner(parts, name):
    moves = []
    for n in range(4):
        moves.append((n, 0, 0, n * 160, 160))
        moves.append((n, 160, 1, n * 288, 288))
    return join(parts, moves, (640, 1152), name)


def dequantize(where_ref, ref, scale_ref, w_ref, first, outer_axis, r, blocks, rows):
    last = 16 * blocks
    pad = rows - last
    codes = jnp.concatenate([ref[n * rows + last : (n + 1) * rows, :] for n in range(16)], axis=0)
    row_kind = jnp.bitwise_and(lax.broadcasted_iota(I32, codes.shape, 0), pad - 1)
    scale_ref[...] = jnp.where(
        row_kind < blocks, decode_scale(codes), codes.astype(F32) * (1.0 / 128.0)
    )
    outer = (where_ref[outer_axis] + r) % 4
    outer_step, inner_step = (1024, 256) if outer_axis == X else (256, 1024)
    inner = where_ref[Y if outer_axis == X else X]

    def one(n, carry):
        inner_at = (inner + n // 4) % 4
        slot_at = (where_ref[Z] + n % 4) % 4
        row = pl.multiple_of(outer * outer_step + inner_at * inner_step + slot_at * 64, 64)
        base = pl.multiple_of(n * rows, 8)
        tail = scale_ref[pl.ds(pl.multiple_of(n * pad, 8), pad), :]
        for b in range(blocks):
            words = ref[pl.ds(base + 16 * b, 16), :]
            scale = jnp.broadcast_to(tail[b : b + 1], (16, 128))
            zero = jnp.broadcast_to(tail[blocks + b : blocks + b + 1], (16, 128))
            at = slice(first + b * 128, first + (b + 1) * 128)
            for i in range(4):
                code = jnp.bitwise_and(jnp.right_shift(words, 4 * i), 15).astype(F32)
                w_ref[pl.ds(row + 16 * i, 16), at] = ((code - zero) * scale).astype(BF16)
        return carry

    lax.fori_loop(0, 16, one, 0, unroll=4)


def rope(x, cosine, sine):
    return x * cosine + pltpu.roll(x, 64, 1) * sine


class Inputs:
    def __init__(self, sources, buffers, semaphores, order):
        self.buffers, self.order = buffers, order
        self.copies = [
            pltpu.make_async_copy(source, buffers[n], semaphores.at[n])
            for n, source in enumerate(sources)
        ]
        for n in order:
            self.copies[n].start()

    def take(self, n):
        self.copies[n].wait()
        return self.buffers[n]


ORDER = (0, 1, 2, 3, 4, 8, 5, 6, 7)


def project_kv_kernel(where_ref, *refs):
    sources, (low_ref, up_ref, cos_ref, sin_ref, out_ref) = refs[:9], refs[9:14]
    buffers, (scale_ref, w_ref, semaphores) = refs[14:23], refs[23:]
    inputs = Inputs(sources, buffers, semaphores, ORDER)
    for r in range(4):
        dequantize(where_ref, inputs.take(r), scale_ref, w_ref, 0, X, r, 2, 40)
    for r in range(4):
        dequantize(where_ref, inputs.take(4 + r), scale_ref, w_ref, 256, Y, r, 2, 40)
    x_ref = inputs.take(8)
    k = jnp.dot(x_ref[...], w_ref[:, :256], preferred_element_type=F32).astype(BF16).astype(F32)
    for h in range(2):
        at = slice(h * 128, (h + 1) * 128)
        out_ref[:, at] = rope(k[:, at], cos_ref[...], sin_ref[...]).astype(BF16)
    v = jnp.dot(x_ref[...], w_ref[:, 256:], preferred_element_type=F32).astype(BF16).astype(F32)
    add = jnp.dot(low_ref[:, 64:128], up_ref[...], preferred_element_type=F32)
    out_ref[:, 256:512] = (v + SCALE * add).astype(BF16)


def project_q_first_kernel(where_ref, *refs):
    sources, out_ref = refs[:7], refs[7]
    buffers, (scale_ref, w_ref, semaphores) = refs[8:15], refs[15:]
    inputs = Inputs(sources, buffers, semaphores, (0, 1, 2, 3, 4, 5, 6))
    x_at = pl.multiple_of((where_ref[X] + 2) % 4 * 1024, 1024)
    y_at = pl.multiple_of((where_ref[Y] + 2) % 4 * 256, 256)
    w_ref[pl.ds(x_at, 1024), :512] = jnp.zeros((1024, 512), BF16)
    for n in range(4):
        w_ref[pl.ds(n * 1024 + y_at, 256), 512:] = jnp.zeros((256, 512), BF16)
    for n, r in enumerate((0, 1, 3)):
        dequantize(where_ref, inputs.take(n), scale_ref, w_ref, 0, X, r, 4, 72)
    for n, r in enumerate((0, 1, 3)):
        dequantize(where_ref, inputs.take(3 + n), scale_ref, w_ref, 512, Y, r, 4, 72)
    x_ref = inputs.take(6)
    for t in range(4):
        at = slice(t * 256, (t + 1) * 256)
        out_ref[:, at] = jnp.dot(x_ref[...], w_ref[:, at], preferred_element_type=F32)


def project_q_last_kernel(where_ref, *refs):
    sources, (low_ref, up_ref, cos_ref, sin_ref, out_ref) = refs[:4], refs[4:9]
    buffers, (scale_ref, w_ref, semaphores) = refs[9:13], refs[13:]
    inputs = Inputs(sources, buffers, semaphores, (0, 1, 2, 3))
    x_at = pl.multiple_of((where_ref[X] + 2) % 4 * 1024, 1024)
    y_at = pl.multiple_of((where_ref[Y] + 2) % 4 * 256, 256)
    dequantize(where_ref, inputs.take(0), scale_ref, w_ref, 0, X, 2, 4, 72)
    dequantize(where_ref, inputs.take(1), scale_ref, w_ref, 512, Y, 2, 4, 72)
    x_ref, sum_ref = inputs.take(2), inputs.take(3)
    for t in range(4):
        at = slice(t * 256, (t + 1) * 256)
        q = sum_ref[:, at]
        if t < 2:
            q = q + jnp.dot(
                x_ref[:, pl.ds(x_at, 1024)],
                w_ref[pl.ds(x_at, 1024), at],
                preferred_element_type=F32,
            )
        else:
            for n in range(4):
                rows = pl.ds(pl.multiple_of(n * 1024 + y_at, 256), 256)
                q = q + jnp.dot(x_ref[:, rows], w_ref[rows, at], preferred_element_type=F32)
        q = q.astype(BF16).astype(F32)
        add = jnp.dot(low_ref[:, 0:64], up_ref[:, at], preferred_element_type=F32)
        q = q + SCALE * add
        for h in range(2):
            at = slice(t * 256 + h * 128, t * 256 + (h + 1) * 128)
            out_ref[:, at] = rope(
                q[:, h * 128 : (h + 1) * 128], cos_ref[...], sin_ref[...]
            ).astype(BF16)


def project(kernel, columns, held_as, where, sources, rest, name):
    full = pl.BlockSpec(memory_space=pltpu.VMEM)
    return pl.pallas_call(
        kernel,
        in_specs=[pl.BlockSpec(memory_space=pltpu.SMEM)]
        + [pl.BlockSpec(memory_space=pl.ANY)] * len(sources)
        + [full] * len(rest),
        out_specs=full,
        out_shape=jax.ShapeDtypeStruct((512, columns), held_as),
        scratch_shapes=[pltpu.VMEM(array.shape, array.dtype) for array in sources]
        + [
            pltpu.VMEM((128, 128), F32),
            pltpu.VMEM((4096, columns), BF16),
            pltpu.SemaphoreType.DMA((len(sources),)),
        ],
        compiler_params=pltpu.CompilerParams(vmem_limit_bytes=60 * 1024 * 1024),
        cost_estimate=cost(6e9, 12e6),
        name=name,
    )(where, *sources, *rest)


def attention_kernel(
    piece_ref,
    q_ref,
    g_ref,
    own_ref,
    other_ref,
    start_ref,
    cos_ref,
    sin_ref,
    out_ref,
    dq_ref,
    dv_own_ref,
    dv_other_ref,
    kv_ref,
    dv_ref,
):
    head, step = pl.program_id(0), pl.program_id(1)

    @pl.when((head == 0) & (step == 0))
    def _():
        for n in range(4):
            at = pl.multiple_of(piece_ref[n] * 128, 128)
            kv_ref[pl.ds(at, 128), :] = own_ref[n * 128 : (n + 1) * 128, :]
            at = pl.multiple_of(piece_ref[4 + n] * 128, 128)
            kv_ref[pl.ds(at, 128), :] = other_ref[n * 128 : (n + 1) * 128, :]

    @pl.when(step == 0)
    def _():
        dv_ref[...] = jnp.zeros_like(dv_ref)

    piece = piece_ref[step]
    first_piece = piece_ref[8 + step]
    first = pl.multiple_of(first_piece * 128, 128)
    q = jnp.concatenate([q_ref[:, i * 128 : (i + 1) * 128] for i in range(4)], axis=0)
    g = jnp.concatenate([g_ref[:, i * 128 : (i + 1) * 128] for i in range(4)], axis=0)
    across = (((1,), (1,)), ((), ()))

    def keys(width):
        at = pl.ds(first, width)
        k = kv_ref[at, pl.ds(pl.multiple_of(head * 128, 128), 128)]
        v = kv_ref[at, pl.ds(pl.multiple_of(256 + head * 128, 128), 128)]
        key_at = first + lax.broadcasted_iota(I32, (128, width), 1)
        query_at = piece * 128 + lax.broadcasted_iota(I32, (128, width), 0)
        allowed = (key_at >= start_ref[...]) & (key_at <= query_at)
        bias = jnp.where(allowed, 0.0, -1e30)
        bias = jnp.concatenate([bias] * 4, axis=0)
        lows = []
        for n in range(1):
            some = slice(n * 512, (n + 1) * 512)
            scores = lax.dot_general(q[some], k, across, preferred_element_type=F32)
            scores = scores * (ROOT * LOG2E) + bias
            dp = lax.dot_general(g[some], v, across, preferred_element_type=F32)
            top = jnp.max(scores, axis=-1, keepdims=True)
            e = jnp.exp2(scores - top)
            p = e * (1.0 / jnp.sum(e, axis=-1, keepdims=True))
            low = p.astype(BF16)
            lows.append(low)
            out = jnp.dot(low, v, preferred_element_type=F32).astype(BF16)
            row = jnp.sum(p * dp, axis=-1, keepdims=True)
            ds = ((p * ROOT) * (dp - row)).astype(BF16)
            dq = jnp.dot(ds, k, preferred_element_type=F32)
            for i in range(4):
                to = slice((n * 4 + i) * 128, (n * 4 + i + 1) * 128)
                rows = slice(i * 128, (i + 1) * 128)
                out_ref[:, to] = out[rows]
                dq_ref[:, to] = rope(dq[rows], cos_ref[...], -sin_ref[...]).astype(BF16)
        dv_ref[at, :] += lax.dot_general(
            jnp.concatenate(lows, axis=0), g, (((0,), (0,)), ((), ())), preferred_element_type=F32
        )

    for count in range(1, 6):
        pl.when(piece - first_piece == count - 1)(functools.partial(keys, count * 128))

    @pl.when(step == 3)
    def _():
        for n in range(4):
            at = pl.multiple_of(piece_ref[n] * 128, 128)
            dv_own_ref[n * 128 : (n + 1) * 128, :] = dv_ref[pl.ds(at, 128), :]
            at = pl.multiple_of(piece_ref[4 + n] * 128, 128)
            dv_other_ref[n * 128 : (n + 1) * 128, :] = dv_ref[pl.ds(at, 128), :].astype(BF16)


def attend(pieces, q, g, own, other, starts, cosine, sine):
    block = pl.BlockSpec((128, 512), lambda h, s, p: (s, h))
    whole = pl.BlockSpec((512, 512), lambda h, s, p: (0, 0))
    rows = pl.BlockSpec((128, 128), lambda h, s, p: (s, 0))
    head = pl.BlockSpec((512, 128), lambda h, s, p: (0, h))
    return pl.pallas_call(
        attention_kernel,
        grid_spec=pltpu.PrefetchScalarGridSpec(
            num_scalar_prefetch=1,
            grid=(2, 4),
            in_specs=[
                block,
                block,
                whole,
                whole,
                pl.BlockSpec((128, 1), lambda h, s, p: (s, 0)),
                rows,
                rows,
            ],
            out_specs=[block, block, head, head],
            scratch_shapes=[pltpu.VMEM((1024, 512), BF16), pltpu.VMEM((1024, 128), F32)],
        ),
        out_shape=[
            jax.ShapeDtypeStruct((512, 1024), BF16),
            jax.ShapeDtypeStruct((512, 1024), BF16),
            jax.ShapeDtypeStruct((512, 256), F32),
            jax.ShapeDtypeStruct((512, 256), BF16),
        ],
        compiler_params=pltpu.CompilerParams(vmem_limit_bytes=VMEM),
        name="attention",
    )(pieces, q, g, own, other, starts, cosine, sine)


def place_up_kernel(core_ref, own_ref, other_ref, q_ref, v_ref):
    for ref, core in ((own_ref, core_ref[0]), (other_ref, 1 - core_ref[0])):
        for b in range(10):
            out, at = (q_ref, core * 1024 + b * 128) if b < 8 else (v_ref, core * 256 + b * 128 - 1024)
            out[:, pl.ds(pl.multiple_of(at, 128), 128)] = ref[b * 64 : (b + 1) * 64, :]


def place_up(core, own, other):
    full = pl.BlockSpec(memory_space=pltpu.VMEM)
    return pl.pallas_call(
        place_up_kernel,
        in_specs=[pl.BlockSpec(memory_space=pltpu.SMEM), full, full],
        out_specs=[full, full],
        out_shape=[
            jax.ShapeDtypeStruct((64, 2048), F32),
            jax.ShapeDtypeStruct((64, 512), F32),
        ],
        name="place_up",
    )(core, own, other)


def on_device(hidden, gain, words, scale_zeros, down, query_up, value_up, documents, cotangent):
    f = lax.axis_index("fsdp")
    c = lax.axis_index("ctx")
    x, y, z = f // 16, f // 4 % 4, f % 4
    pair, core = c // 2, c % 2
    where = jnp.stack([x, y, z]).astype(I32)

    with jax.named_scope("pack_words"):
        packed = pack(core[None].astype(I32), words, scale_zeros)
    with jax.named_scope("gather_z"):
        slots = gather_axis(packed, Z)
    with jax.named_scope("norm"):
        wide = hidden[0].astype(F32)
        mean_square = jnp.mean(wide * wide, axis=-1, keepdims=True)
        normed = (wide * lax.rsqrt(mean_square + EPS) * gain.astype(F32)).astype(BF16)
        normed_other = take_from(normed, CORE, 1)
    with jax.named_scope("gather_inner"):
        *slots, normed_other = lax.optimization_barrier((*slots, normed_other))
        part_a, part_b = join_slots(slots)
        part_a, part_b = gather_axis(part_a, Y), gather_axis(part_b, X)
    with jax.named_scope("permute_features"):
        permuted, some = permute_features(normed, normed_other, core)
        part_a, part_b, permuted, some = lax.optimization_barrier(
            (part_a, part_b, permuted, some)
        )
    with jax.named_scope("gather_outer"):
        kv_a, q_a = join_inner(part_a, "join_y")
        kv_b, q_b = join_inner(part_b, "join_x")
        kv_a, q_a, kv_b, q_b = lax.optimization_barrier((kv_a, q_a, kv_b, q_b))
        kv_a, kv_b = gather_axis(kv_a, X), gather_axis(kv_b, Y)
        near_a = [q_a] + [take_from(q_a, X, r) for r in (1, 3)]
        near_b = [q_b] + [take_from(q_b, Y, r) for r in (1, 3)]

    with jax.named_scope("adapter_in"):
        low = jnp.concatenate(
            [
                jnp.dot(n, down, preferred_element_type=F32).astype(BF16)
                for n in (normed, normed_other)
            ],
            axis=0,
        )
    up_q = lax.dynamic_slice_in_dim(query_up, core * 1024, 1024, 1)
    up_v = lax.dynamic_slice_in_dim(value_up, core * 256, 256, 1)
    with jax.named_scope("tables"):
        c_pair = (1 - pair) * 2 + core
        pieces = jnp.stack(
            [
                c,
                7 - c,
                c ^ 1,
                7 - (c ^ 1),
                c_pair,
                7 - c_pair,
                c_pair ^ 1,
                7 - (c_pair ^ 1),
            ]
        ).astype(I32)
        at = (pieces[:4, None] * 128 + jnp.arange(128, dtype=I32)[None, :]).reshape(512)
        angles = at.astype(F32)[:, None] * frequencies()[None, :]
        cosine, sine = jnp.cos(angles), jnp.sin(angles)
        cosine = jnp.concatenate([cosine, cosine], axis=1)
        sine = jnp.concatenate([-sine, sine], axis=1)
        docs = documents[0]
        spot = jnp.arange(1024, dtype=I32)
        fresh = jnp.concatenate([jnp.ones((1,), bool), docs[1:] != docs[:-1]])
        start = lax.cummax(jnp.where(fresh, spot, 0))
        start = start.reshape(8, 128)
        starts = jnp.concatenate(
            [lax.dynamic_slice_in_dim(start, pieces[n], 1, 0) for n in range(4)], axis=0
        )
        pieces = jnp.concatenate([pieces, starts[:, 0] // 128])
        starts = starts.reshape(512, 1)

    with jax.named_scope("project_kv"):
        kv = project(
            project_kv_kernel,
            512,
            BF16,
            where,
            [*kv_a, *kv_b, permuted],
            (low, up_v, cosine, sine),
            "project_kv",
        )
        kv, q_a, q_b = lax.optimization_barrier((kv, q_a, q_b))
    with jax.named_scope("gather_opposite"):
        far_a, far_b = take_from(q_a, X, 2), take_from(q_b, Y, 2)
        kv_other = take_from(kv, PAIR, 1)
    with jax.named_scope("project_q"):
        total = project(
            project_q_first_kernel,
            1024,
            F32,
            where,
            [*near_a, *near_b, permuted],
            (),
            "project_q_first",
        )
        total, cotangent = lax.optimization_barrier((total, cotangent))
        q = project(
            project_q_last_kernel,
            1024,
            BF16,
            where,
            [far_a, far_b, permuted, total],
            (low, up_q, cosine, sine),
            "project_q_last",
        )
    with jax.named_scope("cotangent_heads"):
        g = cotangent[0]
        g_own = lax.dynamic_slice_in_dim(g, core * 1024, 1024, 1)
        g_other = take_from(lax.dynamic_slice_in_dim(g, (1 - core) * 1024, 1024, 1), CORE, 1)
        g = jnp.concatenate([g_own, g_other], axis=0)

    with jax.named_scope("attention"):
        out, dq, dv_own, dv_other = attend(pieces, q, g, kv, kv_other, starts, cosine, sine)
    with jax.named_scope("context_rows"):
        out_other = take_from(out[256:], CORE, 1)
        context = jnp.concatenate([out[:256], out_other, out[:256]], axis=1)
        context = lax.dynamic_slice_in_dim(context, core * 1024, 2048, 1)[None]
    with jax.named_scope("value_grad"):
        dv = (dv_own + take_from(dv_other, PAIR, 1).astype(F32)).astype(BF16)

    rows_dims = (((0,), (0,)), ((), ()))
    across = (((1,), (1,)), ((), ()))
    with jax.named_scope("adapter_grad"):
        term = jnp.concatenate(
            [
                SCALE * lax.dot_general(dq, up_q, across, preferred_element_type=F32),
                SCALE * lax.dot_general(dv, up_v, across, preferred_element_type=F32),
            ],
            axis=1,
        )
        term_other = take_from(term, CORE, 1)
        low_grad = (term + jnp.concatenate([term_other[256:], term_other[:256]], axis=0)).astype(BF16)
    with jax.named_scope("up_terms"):
        up = jnp.concatenate(
            [
                SCALE * lax.dot_general(low[:, :64], dq, rows_dims, preferred_element_type=F32),
                SCALE * lax.dot_general(low[:, 64:], dv, rows_dims, preferred_element_type=F32),
            ],
            axis=1,
        )
        up = jnp.concatenate([up[:, b * 128 : (b + 1) * 128] for b in range(10)], axis=0)
    with jax.named_scope("down_terms"):
        grad = lax.dot_general(some, low_grad, rows_dims, preferred_element_type=F32)
    with jax.named_scope("sum_plane"):
        parts = jnp.concatenate([grad.reshape(16, 128, 128), up.reshape(16, 40, 128)], axis=1)
        total = jnp.sum(exchange(parts.astype(BF16), PLANE, "fsdp").astype(F32), axis=0)
    with jax.named_scope("sum_z"):
        parts = jnp.concatenate(
            [total[:128].reshape(8, 16, 128), jnp.broadcast_to(total[None, 128:], (8, 40, 128))],
            axis=1,
        )
        total = jnp.sum(exchange(parts, COLUMN, AXES), axis=0)
        grad_down = total[:16]
    with jax.named_scope("share_up"):
        up = exchange(jnp.broadcast_to(total[None, 16:], (16, 40, 128)), PLANE, "fsdp")
        up = up.reshape(640, 128)
        query_up_gradient, value_up_gradient = place_up(
            core[None].astype(I32), up, take_from(up, CORE, 1)
        )
    return context, grad_down, query_up_gradient, value_up_gradient


def solution(mesh):
    return jax.shard_map(
        on_device,
        mesh=mesh,
        in_specs=(
            P("fsdp", "ctx", None),
            P(),
            P("fsdp", None, None),
            P("fsdp", None, None),
            P(),
            P(),
            P(),
            P("fsdp", None),
            P("fsdp", "ctx", None),
        ),
        out_specs=(P("fsdp", "ctx", None), P(("fsdp", "ctx"), None), P(), P()),
        check_vma=False,
    )
```

```python
import functools
import math

import jax
import jax.numpy as jnp
import numpy as np
from jax import lax
from jax.experimental import pallas as pl
from jax.experimental.pallas import tpu as pltpu
from jax.sharding import PartitionSpec as P

HEAD = 128
SCALE = 0.25
EPS = 1e-05
THETA = 500000.0
ROOT = 1.0 / math.sqrt(HEAD)
LOG2E = math.log2(math.e)
AXES = ("fsdp", "ctx")
VMEM = 32 * 1024 * 1024
F32, BF16, I32 = jnp.float32, jnp.bfloat16, jnp.int32


def place(l):
    f, c = divmod(l, 4)
    return [f // 16, f // 4 % 4, f % 4, c // 2, c % 2]


def index(p):
    return ((p[0] * 4 + p[1]) * 4 + p[2]) * 4 + p[3] * 2 + p[4]


SIZES = (4, 4, 4, 2, 2)
X, Y, Z, PAIR, CORE = range(5)


def take_from(value, axis, step):
    pairs = []
    for l in range(256):
        p = place(l)
        p[axis] = (p[axis] - step) % SIZES[axis]
        pairs.append((l, index(p)))
    return lax.ppermute(value, AXES, pairs)


def gather_axis(value, axis):
    return [value] + [take_from(value, axis, r) for r in (1, 2, 3)]


PLANE = [[4 * n + z for n in range(16)] for z in range(4)]
COLUMN = [
    [index((x, y, z, pair, core)) for z in range(4) for pair in range(2)]
    for x in range(4)
    for y in range(4)
    for core in range(2)
]


def exchange(parts, groups, axes):
    return lax.all_to_all(parts, axes, 0, 0, tiled=True, axis_index_groups=groups)


def frequencies():
    exponent = jnp.arange(0, HEAD, 2, dtype=F32) / HEAD
    inverse = 1.0 / THETA**exponent
    wavelength = 2.0 * math.pi / inverse
    blend = (8192.0 / wavelength - 1.0) / 3.0
    middle = (1.0 - blend) * inverse / 8.0 + blend * inverse
    return jnp.where(
        wavelength < 2048.0, inverse, jnp.where(wavelength > 8192.0, inverse / 8.0, middle)
    )


def scale_code(scale):
    m = scale.astype(F32) * 16.0
    e = jnp.full(m.shape, 4, I32)
    for k in (64, 64, 32, 16, 8, 4, 2, 1):
        small = m < 2.0 ** (8 - k)
        m = jnp.where(small, m * 2.0**k, m)
        e = jnp.where(small, e + k, e)
    return m.astype(I32) + 256 * e


def decode_scale(code):
    s = jnp.bitwise_and(code, 255).astype(F32)
    e = jnp.right_shift(code, 8)
    for k in (1, 2, 4, 8, 16, 32, 64):
        s = jnp.where(jnp.bitwise_and(e, k) != 0, s * 2.0**-k, s)
    return jnp.where(jnp.bitwise_and(e, 128) != 0, (s * 2.0**-64) * 2.0**-64, s)


def cost(flops, moved):
    return pl.CostEstimate(flops=int(flops), bytes_accessed=int(moved), transcendentals=0)


def pack_kernel(core_ref, words_ref, params_ref, out_ref):
    core = core_ref[0]
    row = 0
    for first, step, blocks, pad in (
        (2048, 256, 2, 4),
        (0, 1024, 4, 0),
        (2560, 256, 2, 4),
        (512, 1024, 4, 0),
    ):
        for b in range(blocks):
            at = pl.ds(pl.multiple_of(first + core * step + b * 128, 128), 128)
            out_ref[row + 16 * b : row + 16 * b + 16, :] = words_ref[0, :, at]
            params = params_ref[0, :, at].astype(F32)
            tail = row + 16 * blocks + b
            out_ref[tail : tail + 1, :] = scale_code(params[0:1])
            out_ref[tail + blocks : tail + blocks + 1, :] = (params[1:2] * 128.0).astype(I32)
        row += 18 * blocks
        if pad:
            out_ref[row : row + pad, :] = jnp.zeros((pad, 128), I32)
            row += pad


def pack(core, words, params):
    full = pl.BlockSpec(memory_space=pltpu.VMEM)
    return pl.pallas_call(
        pack_kernel,
        in_specs=[pl.BlockSpec(memory_space=pltpu.SMEM), full, full],
        out_specs=full,
        out_shape=jax.ShapeDtypeStruct((224, 128), I32),
        name="pack_words",
    )(core, words, params)


def permute_kernel(own_ref, other_ref, p_ref, half_ref, out_ref, some_ref):
    p, half = p_ref[...], half_ref[...]
    for rows, ref in ((slice(0, 256), own_ref), (slice(256, 512), other_ref)):
        for n in range(4):
            x = ref[:, n * 256 : (n + 1) * 256]
            out_ref[rows, n * 256 : (n + 1) * 256] = jnp.dot(
                x, p, preferred_element_type=F32
            ).astype(BF16)
            some_ref[rows, n * 128 : (n + 1) * 128] = jnp.dot(
                x, half, preferred_element_type=F32
            ).astype(BF16)


def permute_features(own, other, core):
    d = np.arange(256)
    source = (d // 64) * 64 + 4 * (d % 16) + (d % 64) // 16
    p = np.zeros((256, 256), np.float32)
    p[source, d] = 1.0
    d = np.arange(128)
    half = np.zeros((2, 256, 128), np.float32)
    for n in range(2):
        half[n, (d // 16) * 32 + n * 16 + d % 16, d] = 1.0
    half = lax.dynamic_index_in_dim(jnp.asarray(half, BF16), core, 0, keepdims=False)
    return pl.pallas_call(
        permute_kernel,
        grid=(4,),
        in_specs=[
            pl.BlockSpec((256, 1024), lambda i: (0, i)),
            pl.BlockSpec((256, 1024), lambda i: (0, i)),
            pl.BlockSpec((256, 256), lambda i: (0, 0)),
            pl.BlockSpec((256, 128), lambda i: (0, 0)),
        ],
        out_specs=[
            pl.BlockSpec((512, 1024), lambda i: (0, i)),
            pl.BlockSpec((512, 512), lambda i: (0, i)),
        ],
        cost_estimate=cost(1.6e9, 1.0e7),
        out_shape=[
            jax.ShapeDtypeStruct((512, 4096), BF16),
            jax.ShapeDtypeStruct((512, 2048), BF16),
        ],
        name="permute_features",
    )(own, other, jnp.asarray(p, BF16), half)


def join_kernel(moves, count, *refs):
    ins, outs, semaphores = refs[:4], refs[4 : 4 + count], refs[4 + count]
    copies = []
    for n, (source, first, target, at, rows) in enumerate(moves):
        copies.append(
            pltpu.make_async_copy(
                ins[source].at[pl.ds(first, rows), :],
                outs[target].at[pl.ds(at, rows), :],
                semaphores.at[n],
            )
        )
        copies[-1].start()
    for copy in copies:
        copy.wait()


def join(parts, moves, sizes, name):
    anywhere = pl.BlockSpec(memory_space=pl.ANY)
    return pl.pallas_call(
        functools.partial(join_kernel, moves, len(sizes)),
        in_specs=[anywhere] * 4,
        out_specs=[anywhere] * len(sizes),
        out_shape=[jax.ShapeDtypeStruct((n, 128), I32) for n in sizes],
        scratch_shapes=[pltpu.SemaphoreType.DMA((len(moves),))],
        compiler_params=pltpu.CompilerParams(vmem_limit_bytes=1024 * 1024),
        cost_estimate=cost(0, 4e6),
        name=name,
    )(*parts)


def join_slots(slots):
    moves = []
    for half in range(2):
        for n in range(4):
            moves.append((n, half * 112, half, n * 40, 40))
            moves.append((n, half * 112 + 40, half, 160 + n * 72, 72))
    return join(slots, moves, (448, 448), "join_z")


def join_inner(parts, name):
    moves = []
    for n in range(4):
        moves.append((n, 0, 0, n * 160, 160))
        moves.append((n, 160, 1, n * 288, 288))
    return join(parts, moves, (640, 1152), name)


def dequantize(where_ref, ref, scale_ref, w_ref, first, outer_axis, r, blocks, rows):
    last = 16 * blocks
    pad = rows - last
    codes = jnp.concatenate([ref[n * rows + last : (n + 1) * rows, :] for n in range(16)], axis=0)
    row_kind = jnp.bitwise_and(lax.broadcasted_iota(I32, codes.shape, 0), pad - 1)
    scale_ref[...] = jnp.where(
        row_kind < blocks, decode_scale(codes), codes.astype(F32) * (1.0 / 128.0)
    )
    outer = (where_ref[outer_axis] + r) % 4
    outer_step, inner_step = (1024, 256) if outer_axis == X else (256, 1024)
    inner = where_ref[Y if outer_axis == X else X]

    def one(n, carry):
        inner_at = (inner + n // 4) % 4
        slot_at = (where_ref[Z] + n % 4) % 4
        row = pl.multiple_of(outer * outer_step + inner_at * inner_step + slot_at * 64, 64)
        base = pl.multiple_of(n * rows, 8)
        tail = scale_ref[pl.ds(pl.multiple_of(n * pad, 8), pad), :]
        for b in range(blocks):
            words = ref[pl.ds(base + 16 * b, 16), :]
            scale = jnp.broadcast_to(tail[b : b + 1], (16, 128))
            zero = jnp.broadcast_to(tail[blocks + b : blocks + b + 1], (16, 128))
            at = slice(first + b * 128, first + (b + 1) * 128)
            for i in range(4):
                code = jnp.bitwise_and(jnp.right_shift(words, 4 * i), 15).astype(F32)
                w_ref[pl.ds(row + 16 * i, 16), at] = ((code - zero) * scale).astype(BF16)
        return carry

    lax.fori_loop(0, 16, one, 0, unroll=4)


def rope(x, cosine, sine):
    return x * cosine + pltpu.roll(x, 64, 1) * sine


class Inputs:
    def __init__(self, sources, buffers, semaphores, order):
        self.buffers, self.order = buffers, order
        self.copies = [
            pltpu.make_async_copy(source, buffers[n], semaphores.at[n])
            for n, source in enumerate(sources)
        ]
        for n in order:
            self.copies[n].start()

    def take(self, n):
        self.copies[n].wait()
        return self.buffers[n]


ORDER = (0, 1, 2, 3, 4, 8, 5, 6, 7)


def project_kv_kernel(where_ref, *refs):
    sources, (low_ref, up_ref, cos_ref, sin_ref, out_ref) = refs[:9], refs[9:14]
    buffers, (scale_ref, w_ref, semaphores) = refs[14:23], refs[23:]
    inputs = Inputs(sources, buffers, semaphores, ORDER)
    for r in range(4):
        dequantize(where_ref, inputs.take(r), scale_ref, w_ref, 0, X, r, 2, 40)
    for r in range(4):
        dequantize(where_ref, inputs.take(4 + r), scale_ref, w_ref, 256, Y, r, 2, 40)
    x_ref = inputs.take(8)
    k = jnp.dot(x_ref[...], w_ref[:, :256], preferred_element_type=F32).astype(BF16).astype(F32)
    for h in range(2):
        at = slice(h * 128, (h + 1) * 128)
        out_ref[:, at] = rope(k[:, at], cos_ref[...], sin_ref[...]).astype(BF16)
    v = jnp.dot(x_ref[...], w_ref[:, 256:], preferred_element_type=F32).astype(BF16).astype(F32)
    add = jnp.dot(low_ref[:, 64:128], up_ref[...], preferred_element_type=F32)
    out_ref[:, 256:512] = (v + SCALE * add).astype(BF16)


def project_q_kernel(where_ref, *refs):
    sources, (low_ref, up_ref, cos_ref, sin_ref, out_ref) = refs[:9], refs[9:14]
    buffers, (scale_ref, w_ref, semaphores) = refs[14:23], refs[23:]
    inputs = Inputs(sources, buffers, semaphores, ORDER)
    for r in range(4):
        dequantize(where_ref, inputs.take(r), scale_ref, w_ref, 0, X, r, 4, 72)
    for r in range(4):
        dequantize(where_ref, inputs.take(4 + r), scale_ref, w_ref, 512, Y, r, 4, 72)
    x_ref = inputs.take(8)
    for t in range(4):
        at = slice(t * 256, (t + 1) * 256)
        q = jnp.dot(x_ref[...], w_ref[:, at], preferred_element_type=F32).astype(BF16).astype(F32)
        add = jnp.dot(low_ref[:, 0:64], up_ref[:, at], preferred_element_type=F32)
        q = q + SCALE * add
        for h in range(2):
            at = slice(t * 256 + h * 128, t * 256 + (h + 1) * 128)
            out_ref[:, at] = rope(
                q[:, h * 128 : (h + 1) * 128], cos_ref[...], sin_ref[...]
            ).astype(BF16)


def project(kernel, columns, held_as, where, sources, rest, name):
    full = pl.BlockSpec(memory_space=pltpu.VMEM)
    return pl.pallas_call(
        kernel,
        in_specs=[pl.BlockSpec(memory_space=pltpu.SMEM)]
        + [pl.BlockSpec(memory_space=pl.ANY)] * len(sources)
        + [full] * len(rest),
        out_specs=full,
        out_shape=jax.ShapeDtypeStruct((512, columns), held_as),
        scratch_shapes=[pltpu.VMEM(array.shape, array.dtype) for array in sources]
        + [
            pltpu.VMEM((128, 128), F32),
            pltpu.VMEM((4096, columns), BF16),
            pltpu.SemaphoreType.DMA((len(sources),)),
        ],
        compiler_params=pltpu.CompilerParams(vmem_limit_bytes=VMEM),
        cost_estimate=cost(6e9, 12e6),
        name=name,
    )(where, *sources, *rest)


def attention_kernel(
    piece_ref,
    q_ref,
    g_ref,
    own_ref,
    other_ref,
    start_ref,
    cos_ref,
    sin_ref,
    out_ref,
    dq_ref,
    dv_own_ref,
    dv_other_ref,
    kv_ref,
    dv_ref,
):
    head, step = pl.program_id(0), pl.program_id(1)

    @pl.when((head == 0) & (step == 0))
    def _():
        for n in range(4):
            at = pl.multiple_of(piece_ref[n] * 128, 128)
            kv_ref[pl.ds(at, 128), :] = own_ref[n * 128 : (n + 1) * 128, :]
            at = pl.multiple_of(piece_ref[4 + n] * 128, 128)
            kv_ref[pl.ds(at, 128), :] = other_ref[n * 128 : (n + 1) * 128, :]

    @pl.when(step == 0)
    def _():
        dv_ref[...] = jnp.zeros_like(dv_ref)

    piece = piece_ref[step]
    first_piece = piece_ref[8 + step]
    first = pl.multiple_of(first_piece * 128, 128)
    q = jnp.concatenate([q_ref[:, i * 128 : (i + 1) * 128] for i in range(4)], axis=0)
    g = jnp.concatenate([g_ref[:, i * 128 : (i + 1) * 128] for i in range(4)], axis=0)
    across = (((1,), (1,)), ((), ()))

    def keys(width):
        at = pl.ds(first, width)
        k = kv_ref[at, pl.ds(pl.multiple_of(head * 128, 128), 128)]
        v = kv_ref[at, pl.ds(pl.multiple_of(256 + head * 128, 128), 128)]
        key_at = first + lax.broadcasted_iota(I32, (128, width), 1)
        query_at = piece * 128 + lax.broadcasted_iota(I32, (128, width), 0)
        allowed = (key_at >= start_ref[...]) & (key_at <= query_at)
        bias = jnp.where(allowed, 0.0, -1e30)
        bias = jnp.concatenate([bias] * 4, axis=0)
        lows = []
        for n in range(1):
            some = slice(n * 512, (n + 1) * 512)
            scores = lax.dot_general(q[some], k, across, preferred_element_type=F32)
            scores = scores * (ROOT * LOG2E) + bias
            dp = lax.dot_general(g[some], v, across, preferred_element_type=F32)
            top = jnp.max(scores, axis=-1, keepdims=True)
            e = jnp.exp2(scores - top)
            p = e * (1.0 / jnp.sum(e, axis=-1, keepdims=True))
            low = p.astype(BF16)
            lows.append(low)
            out = jnp.dot(low, v, preferred_element_type=F32).astype(BF16)
            row = jnp.sum(p * dp, axis=-1, keepdims=True)
            ds = ((p * ROOT) * (dp - row)).astype(BF16)
            dq = jnp.dot(ds, k, preferred_element_type=F32)
            for i in range(4):
                to = slice((n * 4 + i) * 128, (n * 4 + i + 1) * 128)
                rows = slice(i * 128, (i + 1) * 128)
                out_ref[:, to] = out[rows]
                dq_ref[:, to] = rope(dq[rows], cos_ref[...], -sin_ref[...]).astype(BF16)
        dv_ref[at, :] += lax.dot_general(
            jnp.concatenate(lows, axis=0), g, (((0,), (0,)), ((), ())), preferred_element_type=F32
        )

    for count in range(1, 6):
        pl.when(piece - first_piece == count - 1)(functools.partial(keys, count * 128))

    @pl.when(step == 3)
    def _():
        for n in range(4):
            at = pl.multiple_of(piece_ref[n] * 128, 128)
            dv_own_ref[n * 128 : (n + 1) * 128, :] = dv_ref[pl.ds(at, 128), :]
            at = pl.multiple_of(piece_ref[4 + n] * 128, 128)
            dv_other_ref[n * 128 : (n + 1) * 128, :] = dv_ref[pl.ds(at, 128), :].astype(BF16)


def attend(pieces, q, g, own, other, starts, cosine, sine):
    block = pl.BlockSpec((128, 512), lambda h, s, p: (s, h))
    whole = pl.BlockSpec((512, 512), lambda h, s, p: (0, 0))
    rows = pl.BlockSpec((128, 128), lambda h, s, p: (s, 0))
    head = pl.BlockSpec((512, 128), lambda h, s, p: (0, h))
    return pl.pallas_call(
        attention_kernel,
        grid_spec=pltpu.PrefetchScalarGridSpec(
            num_scalar_prefetch=1,
            grid=(2, 4),
            in_specs=[
                block,
                block,
                whole,
                whole,
                pl.BlockSpec((128, 1), lambda h, s, p: (s, 0)),
                rows,
                rows,
            ],
            out_specs=[block, block, head, head],
            scratch_shapes=[pltpu.VMEM((1024, 512), BF16), pltpu.VMEM((1024, 128), F32)],
        ),
        out_shape=[
            jax.ShapeDtypeStruct((512, 1024), BF16),
            jax.ShapeDtypeStruct((512, 1024), BF16),
            jax.ShapeDtypeStruct((512, 256), F32),
            jax.ShapeDtypeStruct((512, 256), BF16),
        ],
        compiler_params=pltpu.CompilerParams(vmem_limit_bytes=VMEM),
        name="attention",
    )(pieces, q, g, own, other, starts, cosine, sine)


def place_up_kernel(core_ref, own_ref, other_ref, q_ref, v_ref):
    for ref, core in ((own_ref, core_ref[0]), (other_ref, 1 - core_ref[0])):
        for b in range(10):
            out, at = (q_ref, core * 1024 + b * 128) if b < 8 else (v_ref, core * 256 + b * 128 - 1024)
            out[:, pl.ds(pl.multiple_of(at, 128), 128)] = ref[b * 64 : (b + 1) * 64, :]


def place_up(core, own, other):
    full = pl.BlockSpec(memory_space=pltpu.VMEM)
    return pl.pallas_call(
        place_up_kernel,
        in_specs=[pl.BlockSpec(memory_space=pltpu.SMEM), full, full],
        out_specs=[full, full],
        out_shape=[
            jax.ShapeDtypeStruct((64, 2048), F32),
            jax.ShapeDtypeStruct((64, 512), F32),
        ],
        name="place_up",
    )(core, own, other)


def on_device(hidden, gain, words, scale_zeros, down, query_up, value_up, documents, cotangent):
    f = lax.axis_index("fsdp")
    c = lax.axis_index("ctx")
    x, y, z = f // 16, f // 4 % 4, f % 4
    pair, core = c // 2, c % 2
    where = jnp.stack([x, y, z]).astype(I32)

    with jax.named_scope("pack_words"):
        packed = pack(core[None].astype(I32), words, scale_zeros)
    with jax.named_scope("gather_z"):
        slots = gather_axis(packed, Z)
    with jax.named_scope("norm"):
        wide = hidden[0].astype(F32)
        mean_square = jnp.mean(wide * wide, axis=-1, keepdims=True)
        normed = (wide * lax.rsqrt(mean_square + EPS) * gain.astype(F32)).astype(BF16)
        normed_other = take_from(normed, CORE, 1)
    with jax.named_scope("gather_inner"):
        *slots, normed_other = lax.optimization_barrier((*slots, normed_other))
        part_a, part_b = join_slots(slots)
        part_a, part_b = gather_axis(part_a, Y), gather_axis(part_b, X)
    with jax.named_scope("permute_features"):
        permuted, some = permute_features(normed, normed_other, core)
        part_a, part_b, permuted, some = lax.optimization_barrier(
            (part_a, part_b, permuted, some)
        )
    with jax.named_scope("gather_outer"):
        kv_a, q_a = join_inner(part_a, "join_y")
        kv_b, q_b = join_inner(part_b, "join_x")
        kv_a, q_a, kv_b, q_b = lax.optimization_barrier((kv_a, q_a, kv_b, q_b))
        kv_a, kv_b = gather_axis(kv_a, X), gather_axis(kv_b, Y)
        q_a, q_b = gather_axis(q_a, X), gather_axis(q_b, Y)
        q_a[1], q_b[1], cotangent = lax.optimization_barrier((q_a[1], q_b[1], cotangent))

    with jax.named_scope("adapter_in"):
        low = jnp.concatenate(
            [
                jnp.dot(n, down, preferred_element_type=F32).astype(BF16)
                for n in (normed, normed_other)
            ],
            axis=0,
        )
    up_q = lax.dynamic_slice_in_dim(query_up, core * 1024, 1024, 1)
    up_v = lax.dynamic_slice_in_dim(value_up, core * 256, 256, 1)
    with jax.named_scope("tables"):
        c_pair = (1 - pair) * 2 + core
        pieces = jnp.stack(
            [
                c,
                7 - c,
                c ^ 1,
                7 - (c ^ 1),
                c_pair,
                7 - c_pair,
                c_pair ^ 1,
                7 - (c_pair ^ 1),
            ]
        ).astype(I32)
        at = (pieces[:4, None] * 128 + jnp.arange(128, dtype=I32)[None, :]).reshape(512)
        angles = at.astype(F32)[:, None] * frequencies()[None, :]
        cosine, sine = jnp.cos(angles), jnp.sin(angles)
        cosine = jnp.concatenate([cosine, cosine], axis=1)
        sine = jnp.concatenate([-sine, sine], axis=1)
        docs = documents[0]
        spot = jnp.arange(1024, dtype=I32)
        fresh = jnp.concatenate([jnp.ones((1,), bool), docs[1:] != docs[:-1]])
        start = lax.cummax(jnp.where(fresh, spot, 0))
        start = start.reshape(8, 128)
        starts = jnp.concatenate(
            [lax.dynamic_slice_in_dim(start, pieces[n], 1, 0) for n in range(4)], axis=0
        )
        pieces = jnp.concatenate([pieces, starts[:, 0] // 128])
        starts = starts.reshape(512, 1)

    with jax.named_scope("project_kv"):
        kv = project(
            project_kv_kernel,
            512,
            BF16,
            where,
            [*kv_a, *kv_b, permuted],
            (low, up_v, cosine, sine),
            "project_kv",
        )
        kv_other = take_from(kv, PAIR, 1)
    with jax.named_scope("project_q"):
        q = project(
            project_q_kernel,
            1024,
            BF16,
            where,
            [*q_a, *q_b, permuted],
            (low, up_q, cosine, sine),
            "project_q",
        )
    with jax.named_scope("cotangent_heads"):
        g = cotangent[0]
        g_own = lax.dynamic_slice_in_dim(g, core * 1024, 1024, 1)
        g_other = take_from(lax.dynamic_slice_in_dim(g, (1 - core) * 1024, 1024, 1), CORE, 1)
        g = jnp.concatenate([g_own, g_other], axis=0)

    with jax.named_scope("attention"):
        out, dq, dv_own, dv_other = attend(pieces, q, g, kv, kv_other, starts, cosine, sine)
    with jax.named_scope("context_rows"):
        out_other = take_from(out[256:], CORE, 1)
        context = jnp.concatenate([out[:256], out_other, out[:256]], axis=1)
        context = lax.dynamic_slice_in_dim(context, core * 1024, 2048, 1)[None]
    with jax.named_scope("value_grad"):
        dv = (dv_own + take_from(dv_other, PAIR, 1).astype(F32)).astype(BF16)

    rows_dims = (((0,), (0,)), ((), ()))
    across = (((1,), (1,)), ((), ()))
    with jax.named_scope("adapter_grad"):
        term = jnp.concatenate(
            [
                SCALE * lax.dot_general(dq, up_q, across, preferred_element_type=F32),
                SCALE * lax.dot_general(dv, up_v, across, preferred_element_type=F32),
            ],
            axis=1,
        )
        term, dq = lax.optimization_barrier((term, dq))
        term_other = take_from(term, CORE, 1)
        low_grad = (term + jnp.concatenate([term_other[256:], term_other[:256]], axis=0)).astype(BF16)
    with jax.named_scope("up_terms"):
        up = jnp.concatenate(
            [
                SCALE * lax.dot_general(low[:, :64], dq, rows_dims, preferred_element_type=F32),
                SCALE * lax.dot_general(low[:, 64:], dv, rows_dims, preferred_element_type=F32),
            ],
            axis=1,
        )
        up = jnp.concatenate([up[:, b * 128 : (b + 1) * 128] for b in range(10)], axis=0)
    with jax.named_scope("down_terms"):
        grad = lax.dot_general(some, low_grad, rows_dims, preferred_element_type=F32)
    with jax.named_scope("sum_plane"):
        parts = jnp.concatenate([grad.reshape(16, 128, 128), up.reshape(16, 40, 128)], axis=1)
        total = jnp.sum(exchange(parts.astype(BF16), PLANE, "fsdp").astype(F32), axis=0)
    with jax.named_scope("sum_z"):
        parts = jnp.concatenate(
            [total[:128].reshape(8, 16, 128), jnp.broadcast_to(total[None, 128:], (8, 40, 128))],
            axis=1,
        )
        parts, context = lax.optimization_barrier((exchange(parts, COLUMN, AXES), context))
        total = jnp.sum(parts, axis=0)
        grad_down = total[:16]
    with jax.named_scope("share_up"):
        up = exchange(jnp.broadcast_to(total[None, 16:], (16, 40, 128)), PLANE, "fsdp")
        up = up.reshape(640, 128)
        query_up_gradient, value_up_gradient = place_up(
            core[None].astype(I32), up, take_from(up, CORE, 1)
        )
    return context, grad_down, query_up_gradient, value_up_gradient


def solution(mesh):
    return jax.shard_map(
        on_device,
        mesh=mesh,
        in_specs=(
            P("fsdp", "ctx", None),
            P(),
            P("fsdp", None, None),
            P("fsdp", None, None),
            P(),
            P(),
            P(),
            P("fsdp", None),
            P("fsdp", "ctx", None),
        ),
        out_specs=(P("fsdp", "ctx", None), P(("fsdp", "ctx"), None), P(), P()),
        check_vma=False,
    )
```

```python
import functools
import math

import jax
import jax.numpy as jnp
import numpy as np
from jax import lax
from jax.experimental import pallas as pl
from jax.experimental.pallas import tpu as pltpu
from jax.sharding import PartitionSpec as P

HEAD = 128
SCALE = 0.25
EPS = 1e-05
THETA = 500000.0
ROOT = 1.0 / math.sqrt(HEAD)
LOG2E = math.log2(math.e)
AXES = ("fsdp", "ctx")
VMEM = 32 * 1024 * 1024
F32, BF16, I32 = jnp.float32, jnp.bfloat16, jnp.int32


def place(l):
    f, c = divmod(l, 4)
    return [f // 16, f // 4 % 4, f % 4, c // 2, c % 2]


def index(p):
    return ((p[0] * 4 + p[1]) * 4 + p[2]) * 4 + p[3] * 2 + p[4]


SIZES = (4, 4, 4, 2, 2)
X, Y, Z, PAIR, CORE = range(5)


def take_from(value, axis, step):
    pairs = []
    for l in range(256):
        p = place(l)
        p[axis] = (p[axis] - step) % SIZES[axis]
        pairs.append((l, index(p)))
    return lax.ppermute(value, AXES, pairs)


def gather_axis(value, axis):
    return [value] + [take_from(value, axis, r) for r in (1, 2, 3)]


PLANE = [[4 * n + z for n in range(16)] for z in range(4)]
COLUMN = [
    [index((x, y, z, pair, core)) for z in range(4) for pair in range(2)]
    for x in range(4)
    for y in range(4)
    for core in range(2)
]


def exchange(parts, groups, axes):
    return lax.all_to_all(parts, axes, 0, 0, tiled=True, axis_index_groups=groups)


def frequencies():
    exponent = jnp.arange(0, HEAD, 2, dtype=F32) / HEAD
    inverse = 1.0 / THETA**exponent
    wavelength = 2.0 * math.pi / inverse
    blend = (8192.0 / wavelength - 1.0) / 3.0
    middle = (1.0 - blend) * inverse / 8.0 + blend * inverse
    return jnp.where(
        wavelength < 2048.0, inverse, jnp.where(wavelength > 8192.0, inverse / 8.0, middle)
    )


def scale_code(scale):
    m = scale.astype(F32) * 16.0
    e = jnp.full(m.shape, 4, I32)
    for k in (64, 64, 32, 16, 8, 4, 2, 1):
        small = m < 2.0 ** (8 - k)
        m = jnp.where(small, m * 2.0**k, m)
        e = jnp.where(small, e + k, e)
    return m.astype(I32) + 256 * e


def decode_scale(code):
    s = jnp.bitwise_and(code, 255).astype(F32)
    e = jnp.right_shift(code, 8)
    for k in (1, 2, 4, 8, 16, 32, 64):
        s = jnp.where(jnp.bitwise_and(e, k) != 0, s * 2.0**-k, s)
    return jnp.where(jnp.bitwise_and(e, 128) != 0, (s * 2.0**-64) * 2.0**-64, s)


def cost(flops, moved):
    return pl.CostEstimate(flops=int(flops), bytes_accessed=int(moved), transcendentals=0)


def pack_kernel(core_ref, words_ref, params_ref, out_ref):
    core = core_ref[0]
    row = 0
    for first, step, blocks, pad in (
        (2048, 256, 2, 4),
        (0, 1024, 4, 0),
        (2560, 256, 2, 4),
        (512, 1024, 4, 0),
    ):
        for b in range(blocks):
            at = pl.ds(pl.multiple_of(first + core * step + b * 128, 128), 128)
            out_ref[row + 16 * b : row + 16 * b + 16, :] = words_ref[0, :, at]
            params = params_ref[0, :, at].astype(F32)
            tail = row + 16 * blocks + b
            out_ref[tail : tail + 1, :] = scale_code(params[0:1])
            out_ref[tail + blocks : tail + blocks + 1, :] = (params[1:2] * 128.0).astype(I32)
        row += 18 * blocks
        if pad:
            out_ref[row : row + pad, :] = jnp.zeros((pad, 128), I32)
            row += pad


def pack(core, words, params):
    full = pl.BlockSpec(memory_space=pltpu.VMEM)
    return pl.pallas_call(
        pack_kernel,
        in_specs=[pl.BlockSpec(memory_space=pltpu.SMEM), full, full],
        out_specs=full,
        out_shape=jax.ShapeDtypeStruct((224, 128), I32),
        name="pack_words",
    )(core, words, params)


def permute_kernel(own_ref, other_ref, p_ref, half_ref, out_ref, some_ref):
    p, half = p_ref[...], half_ref[...]
    for rows, ref in ((slice(0, 256), own_ref), (slice(256, 512), other_ref)):
        for n in range(4):
            x = ref[:, n * 256 : (n + 1) * 256]
            out_ref[rows, n * 256 : (n + 1) * 256] = jnp.dot(
                x, p, preferred_element_type=F32
            ).astype(BF16)
            some_ref[rows, n * 128 : (n + 1) * 128] = jnp.dot(
                x, half, preferred_element_type=F32
            ).astype(BF16)


def permute_features(own, other, core):
    d = np.arange(256)
    source = (d // 64) * 64 + 4 * (d % 16) + (d % 64) // 16
    p = np.zeros((256, 256), np.float32)
    p[source, d] = 1.0
    d = np.arange(128)
    half = np.zeros((2, 256, 128), np.float32)
    for n in range(2):
        half[n, (d // 16) * 32 + n * 16 + d % 16, d] = 1.0
    half = lax.dynamic_index_in_dim(jnp.asarray(half, BF16), core, 0, keepdims=False)
    return pl.pallas_call(
        permute_kernel,
        grid=(4,),
        in_specs=[
            pl.BlockSpec((256, 1024), lambda i: (0, i)),
            pl.BlockSpec((256, 1024), lambda i: (0, i)),
            pl.BlockSpec((256, 256), lambda i: (0, 0)),
            pl.BlockSpec((256, 128), lambda i: (0, 0)),
        ],
        out_specs=[
            pl.BlockSpec((512, 1024), lambda i: (0, i)),
            pl.BlockSpec((512, 512), lambda i: (0, i)),
        ],
        cost_estimate=cost(1.6e9, 1.0e7),
        out_shape=[
            jax.ShapeDtypeStruct((512, 4096), BF16),
            jax.ShapeDtypeStruct((512, 2048), BF16),
        ],
        name="permute_features",
    )(own, other, jnp.asarray(p, BF16), half)


def join_kernel(moves, count, *refs):
    ins, outs, semaphores = refs[:4], refs[4 : 4 + count], refs[4 + count]
    copies = []
    for n, (source, first, target, at, rows) in enumerate(moves):
        copies.append(
            pltpu.make_async_copy(
                ins[source].at[pl.ds(first, rows), :],
                outs[target].at[pl.ds(at, rows), :],
                semaphores.at[n],
            )
        )
        copies[-1].start()
    for copy in copies:
        copy.wait()


def join(parts, moves, sizes, name):
    anywhere = pl.BlockSpec(memory_space=pl.ANY)
    return pl.pallas_call(
        functools.partial(join_kernel, moves, len(sizes)),
        in_specs=[anywhere] * 4,
        out_specs=[anywhere] * len(sizes),
        out_shape=[jax.ShapeDtypeStruct((n, 128), I32) for n in sizes],
        scratch_shapes=[pltpu.SemaphoreType.DMA((len(moves),))],
        compiler_params=pltpu.CompilerParams(vmem_limit_bytes=1024 * 1024),
        cost_estimate=cost(0, 4e6),
        name=name,
    )(*parts)


def join_slots(slots):
    moves = []
    for half in range(2):
        for n in range(4):
            moves.append((n, half * 112, half, n * 40, 40))
            moves.append((n, half * 112 + 40, half, 160 + n * 72, 72))
    return join(slots, moves, (448, 448), "join_z")


def join_inner(parts, name):
    moves = []
    for n in range(4):
        moves.append((n, 0, 0, n * 160, 160))
        moves.append((n, 160, 1, n * 288, 288))
    return join(parts, moves, (640, 1152), name)


def dequantize(where_ref, ref, scale_ref, w_ref, first, outer_axis, r, blocks, rows):
    last = 16 * blocks
    pad = rows - last
    codes = jnp.concatenate([ref[n * rows + last : (n + 1) * rows, :] for n in range(16)], axis=0)
    row_kind = jnp.bitwise_and(lax.broadcasted_iota(I32, codes.shape, 0), pad - 1)
    scale_ref[...] = jnp.where(
        row_kind < blocks, decode_scale(codes), codes.astype(F32) * (1.0 / 128.0)
    )
    outer = (where_ref[outer_axis] + r) % 4
    outer_step, inner_step = (1024, 256) if outer_axis == X else (256, 1024)
    inner = where_ref[Y if outer_axis == X else X]

    def one(n, carry):
        inner_at = (inner + n // 4) % 4
        slot_at = (where_ref[Z] + n % 4) % 4
        row = pl.multiple_of(outer * outer_step + inner_at * inner_step + slot_at * 64, 64)
        base = pl.multiple_of(n * rows, 8)
        tail = scale_ref[pl.ds(pl.multiple_of(n * pad, 8), pad), :]
        for b in range(blocks):
            words = ref[pl.ds(base + 16 * b, 16), :]
            scale = jnp.broadcast_to(tail[b : b + 1], (16, 128))
            zero = jnp.broadcast_to(tail[blocks + b : blocks + b + 1], (16, 128))
            at = slice(first + b * 128, first + (b + 1) * 128)
            for i in range(4):
                code = jnp.bitwise_and(jnp.right_shift(words, 4 * i), 15).astype(F32)
                w_ref[pl.ds(row + 16 * i, 16), at] = ((code - zero) * scale).astype(BF16)
        return carry

    lax.fori_loop(0, 16, one, 0, unroll=4)


def rope(x, cosine, sine):
    return x * cosine + pltpu.roll(x, 64, 1) * sine


class Inputs:
    def __init__(self, sources, buffers, semaphores, order):
        self.buffers, self.order = buffers, order
        self.copies = [
            pltpu.make_async_copy(source, buffers[n], semaphores.at[n])
            for n, source in enumerate(sources)
        ]
        for n in order:
            self.copies[n].start()

    def take(self, n):
        self.copies[n].wait()
        return self.buffers[n]


ORDER = (0, 1, 2, 3, 4, 8, 5, 6, 7)


def project_kv_kernel(where_ref, *refs):
    sources, (low_ref, up_ref, cos_ref, sin_ref, out_ref) = refs[:9], refs[9:14]
    buffers, (scale_ref, w_ref, semaphores) = refs[14:23], refs[23:]
    inputs = Inputs(sources, buffers, semaphores, ORDER)
    for r in range(4):
        dequantize(where_ref, inputs.take(r), scale_ref, w_ref, 0, X, r, 2, 40)
    for r in range(4):
        dequantize(where_ref, inputs.take(4 + r), scale_ref, w_ref, 256, Y, r, 2, 40)
    x_ref = inputs.take(8)
    k = jnp.dot(x_ref[...], w_ref[:, :256], preferred_element_type=F32).astype(BF16).astype(F32)
    for h in range(2):
        at = slice(h * 128, (h + 1) * 128)
        out_ref[:, at] = rope(k[:, at], cos_ref[...], sin_ref[...]).astype(BF16)
    v = jnp.dot(x_ref[...], w_ref[:, 256:], preferred_element_type=F32).astype(BF16).astype(F32)
    add = jnp.dot(low_ref[:, 64:128], up_ref[...], preferred_element_type=F32)
    out_ref[:, 256:512] = (v + SCALE * add).astype(BF16)


def project_q_kernel(where_ref, *refs):
    sources, (low_ref, up_ref, cos_ref, sin_ref, out_ref) = refs[:9], refs[9:14]
    buffers, (scale_ref, w_ref, semaphores) = refs[14:23], refs[23:]
    inputs = Inputs(sources, buffers, semaphores, ORDER)
    for r in range(4):
        dequantize(where_ref, inputs.take(r), scale_ref, w_ref, 0, X, r, 4, 72)
    for r in range(4):
        dequantize(where_ref, inputs.take(4 + r), scale_ref, w_ref, 512, Y, r, 4, 72)
    x_ref = inputs.take(8)
    for t in range(4):
        at = slice(t * 256, (t + 1) * 256)
        q = jnp.dot(x_ref[...], w_ref[:, at], preferred_element_type=F32).astype(BF16).astype(F32)
        add = jnp.dot(low_ref[:, 0:64], up_ref[:, at], preferred_element_type=F32)
        q = q + SCALE * add
        for h in range(2):
            at = slice(t * 256 + h * 128, t * 256 + (h + 1) * 128)
            out_ref[:, at] = rope(
                q[:, h * 128 : (h + 1) * 128], cos_ref[...], sin_ref[...]
            ).astype(BF16)


def project(kernel, columns, held_as, where, sources, rest, name):
    full = pl.BlockSpec(memory_space=pltpu.VMEM)
    return pl.pallas_call(
        kernel,
        in_specs=[pl.BlockSpec(memory_space=pltpu.SMEM)]
        + [pl.BlockSpec(memory_space=pl.ANY)] * len(sources)
        + [full] * len(rest),
        out_specs=full,
        out_shape=jax.ShapeDtypeStruct((512, columns), held_as),
        scratch_shapes=[pltpu.VMEM(array.shape, array.dtype) for array in sources]
        + [
            pltpu.VMEM((128, 128), F32),
            pltpu.VMEM((4096, columns), BF16),
            pltpu.SemaphoreType.DMA((len(sources),)),
        ],
        compiler_params=pltpu.CompilerParams(vmem_limit_bytes=VMEM),
        cost_estimate=cost(6e9, 12e6),
        name=name,
    )(where, *sources, *rest)


def attention_kernel(
    piece_ref,
    q_ref,
    g_ref,
    own_ref,
    other_ref,
    start_ref,
    cos_ref,
    sin_ref,
    out_ref,
    dq_ref,
    dv_own_ref,
    dv_other_ref,
    kv_ref,
    dv_ref,
):
    head, step = pl.program_id(0), pl.program_id(1)

    @pl.when((head == 0) & (step == 0))
    def _():
        for n in range(4):
            at = pl.multiple_of(piece_ref[n] * 128, 128)
            kv_ref[pl.ds(at, 128), :] = own_ref[n * 128 : (n + 1) * 128, :]
            at = pl.multiple_of(piece_ref[4 + n] * 128, 128)
            kv_ref[pl.ds(at, 128), :] = other_ref[n * 128 : (n + 1) * 128, :]

    @pl.when(step == 0)
    def _():
        dv_ref[...] = jnp.zeros_like(dv_ref)

    piece = piece_ref[step]
    first_piece = piece_ref[8 + step]
    first = pl.multiple_of(first_piece * 128, 128)
    q = jnp.concatenate([q_ref[:, i * 128 : (i + 1) * 128] for i in range(4)], axis=0)
    g = jnp.concatenate([g_ref[:, i * 128 : (i + 1) * 128] for i in range(4)], axis=0)
    across = (((1,), (1,)), ((), ()))

    def keys(width):
        at = pl.ds(first, width)
        k = kv_ref[at, pl.ds(pl.multiple_of(head * 128, 128), 128)]
        v = kv_ref[at, pl.ds(pl.multiple_of(256 + head * 128, 128), 128)]
        key_at = first + lax.broadcasted_iota(I32, (128, width), 1)
        query_at = piece * 128 + lax.broadcasted_iota(I32, (128, width), 0)
        allowed = (key_at >= start_ref[...]) & (key_at <= query_at)
        bias = jnp.where(allowed, 0.0, -1e30)
        bias = jnp.concatenate([bias] * 4, axis=0)
        lows = []
        for n in range(1):
            some = slice(n * 512, (n + 1) * 512)
            scores = lax.dot_general(q[some], k, across, preferred_element_type=F32)
            scores = scores * (ROOT * LOG2E) + bias
            dp = lax.dot_general(g[some], v, across, preferred_element_type=F32)
            top = jnp.max(scores, axis=-1, keepdims=True)
            e = jnp.exp2(scores - top)
            p = e * (1.0 / jnp.sum(e, axis=-1, keepdims=True))
            low = p.astype(BF16)
            lows.append(low)
            out = jnp.dot(low, v, preferred_element_type=F32).astype(BF16)
            row = jnp.sum(p * dp, axis=-1, keepdims=True)
            ds = ((p * ROOT) * (dp - row)).astype(BF16)
            dq = jnp.dot(ds, k, preferred_element_type=F32)
            for i in range(4):
                to = slice((n * 4 + i) * 128, (n * 4 + i + 1) * 128)
                rows = slice(i * 128, (i + 1) * 128)
                out_ref[:, to] = out[rows]
                dq_ref[:, to] = rope(dq[rows], cos_ref[...], -sin_ref[...]).astype(BF16)
        dv_ref[at, :] += lax.dot_general(
            jnp.concatenate(lows, axis=0), g, (((0,), (0,)), ((), ())), preferred_element_type=F32
        )

    for count in range(1, 6):
        pl.when(piece - first_piece == count - 1)(functools.partial(keys, count * 128))

    @pl.when(step == 3)
    def _():
        for n in range(4):
            at = pl.multiple_of(piece_ref[n] * 128, 128)
            dv_own_ref[n * 128 : (n + 1) * 128, :] = dv_ref[pl.ds(at, 128), :]
            at = pl.multiple_of(piece_ref[4 + n] * 128, 128)
            dv_other_ref[n * 128 : (n + 1) * 128, :] = dv_ref[pl.ds(at, 128), :].astype(BF16)


def attend(pieces, q, g, own, other, starts, cosine, sine):
    block = pl.BlockSpec((128, 512), lambda h, s, p: (s, h))
    whole = pl.BlockSpec((512, 512), lambda h, s, p: (0, 0))
    rows = pl.BlockSpec((128, 128), lambda h, s, p: (s, 0))
    head = pl.BlockSpec((512, 128), lambda h, s, p: (0, h))
    return pl.pallas_call(
        attention_kernel,
        grid_spec=pltpu.PrefetchScalarGridSpec(
            num_scalar_prefetch=1,
            grid=(2, 4),
            in_specs=[
                block,
                block,
                whole,
                whole,
                pl.BlockSpec((128, 1), lambda h, s, p: (s, 0)),
                rows,
                rows,
            ],
            out_specs=[block, block, head, head],
            scratch_shapes=[pltpu.VMEM((1024, 512), BF16), pltpu.VMEM((1024, 128), F32)],
        ),
        out_shape=[
            jax.ShapeDtypeStruct((512, 1024), BF16),
            jax.ShapeDtypeStruct((512, 1024), BF16),
            jax.ShapeDtypeStruct((512, 256), F32),
            jax.ShapeDtypeStruct((512, 256), BF16),
        ],
        compiler_params=pltpu.CompilerParams(vmem_limit_bytes=VMEM),
        name="attention",
    )(pieces, q, g, own, other, starts, cosine, sine)


def place_up_kernel(core_ref, own_ref, other_ref, q_ref, v_ref):
    for ref, core in ((own_ref, core_ref[0]), (other_ref, 1 - core_ref[0])):
        for b in range(10):
            out, at = (q_ref, core * 1024 + b * 128) if b < 8 else (v_ref, core * 256 + b * 128 - 1024)
            out[:, pl.ds(pl.multiple_of(at, 128), 128)] = ref[b * 64 : (b + 1) * 64, :]


def place_up(core, own, other):
    full = pl.BlockSpec(memory_space=pltpu.VMEM)
    return pl.pallas_call(
        place_up_kernel,
        in_specs=[pl.BlockSpec(memory_space=pltpu.SMEM), full, full],
        out_specs=[full, full],
        out_shape=[
            jax.ShapeDtypeStruct((64, 2048), F32),
            jax.ShapeDtypeStruct((64, 512), F32),
        ],
        name="place_up",
    )(core, own, other)


def on_device(hidden, gain, words, scale_zeros, down, query_up, value_up, documents, cotangent):
    f = lax.axis_index("fsdp")
    c = lax.axis_index("ctx")
    x, y, z = f // 16, f // 4 % 4, f % 4
    pair, core = c // 2, c % 2
    where = jnp.stack([x, y, z]).astype(I32)

    with jax.named_scope("pack_words"):
        packed = pack(core[None].astype(I32), words, scale_zeros)
    with jax.named_scope("gather_z"):
        slots = gather_axis(packed, Z)
    with jax.named_scope("norm"):
        wide = hidden[0].astype(F32)
        mean_square = jnp.mean(wide * wide, axis=-1, keepdims=True)
        normed = (wide * lax.rsqrt(mean_square + EPS) * gain.astype(F32)).astype(BF16)
        normed_other = take_from(normed, CORE, 1)
    with jax.named_scope("gather_inner"):
        *slots, normed_other = lax.optimization_barrier((*slots, normed_other))
        part_a, part_b = join_slots(slots)
        part_a, part_b = gather_axis(part_a, Y), gather_axis(part_b, X)
    with jax.named_scope("permute_features"):
        permuted, some = permute_features(normed, normed_other, core)
        part_a, part_b, permuted, some = lax.optimization_barrier(
            (part_a, part_b, permuted, some)
        )
    with jax.named_scope("gather_outer"):
        kv_a, q_a = join_inner(part_a, "join_y")
        kv_b, q_b = join_inner(part_b, "join_x")
        kv_a, q_a, kv_b, q_b = lax.optimization_barrier((kv_a, q_a, kv_b, q_b))
        kv_a, kv_b = gather_axis(kv_a, X), gather_axis(kv_b, Y)
        q_a, q_b = gather_axis(q_a, X), gather_axis(q_b, Y)
        q_a[3], q_b[3], cotangent = lax.optimization_barrier((q_a[3], q_b[3], cotangent))

    with jax.named_scope("adapter_in"):
        low = jnp.concatenate(
            [
                jnp.dot(n, down, preferred_element_type=F32).astype(BF16)
                for n in (normed, normed_other)
            ],
            axis=0,
        )
    up_q = lax.dynamic_slice_in_dim(query_up, core * 1024, 1024, 1)
    up_v = lax.dynamic_slice_in_dim(value_up, core * 256, 256, 1)
    with jax.named_scope("tables"):
        c_pair = (1 - pair) * 2 + core
        pieces = jnp.stack(
            [
                c,
                7 - c,
                c ^ 1,
                7 - (c ^ 1),
                c_pair,
                7 - c_pair,
                c_pair ^ 1,
                7 - (c_pair ^ 1),
            ]
        ).astype(I32)
        at = (pieces[:4, None] * 128 + jnp.arange(128, dtype=I32)[None, :]).reshape(512)
        angles = at.astype(F32)[:, None] * frequencies()[None, :]
        cosine, sine = jnp.cos(angles), jnp.sin(angles)
        cosine = jnp.concatenate([cosine, cosine], axis=1)
        sine = jnp.concatenate([-sine, sine], axis=1)
        docs = documents[0]
        spot = jnp.arange(1024, dtype=I32)
        fresh = jnp.concatenate([jnp.ones((1,), bool), docs[1:] != docs[:-1]])
        start = lax.cummax(jnp.where(fresh, spot, 0))
        start = start.reshape(8, 128)
        starts = jnp.concatenate(
            [lax.dynamic_slice_in_dim(start, pieces[n], 1, 0) for n in range(4)], axis=0
        )
        pieces = jnp.concatenate([pieces, starts[:, 0] // 128])
        starts = starts.reshape(512, 1)

    with jax.named_scope("project_kv"):
        kv = project(
            project_kv_kernel,
            512,
            BF16,
            where,
            [*kv_a, *kv_b, permuted],
            (low, up_v, cosine, sine),
            "project_kv",
        )
        kv_other = take_from(kv, PAIR, 1)
    with jax.named_scope("project_q"):
        q = project(
            project_q_kernel,
            1024,
            BF16,
            where,
            [*q_a, *q_b, permuted],
            (low, up_q, cosine, sine),
            "project_q",
        )
    with jax.named_scope("cotangent_heads"):
        g = cotangent[0]
        g_own = lax.dynamic_slice_in_dim(g, core * 1024, 1024, 1)
        g_other = take_from(lax.dynamic_slice_in_dim(g, (1 - core) * 1024, 1024, 1), CORE, 1)
        g = jnp.concatenate([g_own, g_other], axis=0)

    with jax.named_scope("attention"):
        out, dq, dv_own, dv_other = attend(pieces, q, g, kv, kv_other, starts, cosine, sine)
    with jax.named_scope("context_rows"):
        out_other = take_from(out[256:], CORE, 1)
        context = jnp.concatenate([out[:256], out_other, out[:256]], axis=1)
        context = lax.dynamic_slice_in_dim(context, core * 1024, 2048, 1)[None]
    with jax.named_scope("value_grad"):
        dv = (dv_own + take_from(dv_other, PAIR, 1).astype(F32)).astype(BF16)

    rows_dims = (((0,), (0,)), ((), ()))
    across = (((1,), (1,)), ((), ()))
    with jax.named_scope("adapter_grad"):
        term = jnp.concatenate(
            [
                SCALE * lax.dot_general(dq, up_q, across, preferred_element_type=F32),
                SCALE * lax.dot_general(dv, up_v, across, preferred_element_type=F32),
            ],
            axis=1,
        )
        term, dq = lax.optimization_barrier((term, dq))
        term_other = take_from(term, CORE, 1)
        low_grad = (term + jnp.concatenate([term_other[256:], term_other[:256]], axis=0)).astype(BF16)
    with jax.named_scope("up_terms"):
        up = jnp.concatenate(
            [
                SCALE * lax.dot_general(low[:, :64], dq, rows_dims, preferred_element_type=F32),
                SCALE * lax.dot_general(low[:, 64:], dv, rows_dims, preferred_element_type=F32),
            ],
            axis=1,
        )
        up = jnp.concatenate([up[:, b * 128 : (b + 1) * 128] for b in range(10)], axis=0)
    with jax.named_scope("down_terms"):
        grad = lax.dot_general(some, low_grad, rows_dims, preferred_element_type=F32)
    with jax.named_scope("sum_plane"):
        parts = jnp.concatenate([grad.reshape(16, 128, 128), up.reshape(16, 40, 128)], axis=1)
        total = jnp.sum(exchange(parts.astype(BF16), PLANE, "fsdp").astype(F32), axis=0)
    with jax.named_scope("sum_z"):
        parts = jnp.concatenate(
            [total[:128].reshape(8, 16, 128), jnp.broadcast_to(total[None, 128:], (8, 40, 128))],
            axis=1,
        )
        parts, context = lax.optimization_barrier((exchange(parts, COLUMN, AXES), context))
        total = jnp.sum(parts, axis=0)
        grad_down = total[:16]
    with jax.named_scope("share_up"):
        up = exchange(jnp.broadcast_to(total[None, 16:], (16, 40, 128)), PLANE, "fsdp")
        up = up.reshape(640, 128)
        query_up_gradient, value_up_gradient = place_up(
            core[None].astype(I32), up, take_from(up, CORE, 1)
        )
    return context, grad_down, query_up_gradient, value_up_gradient


def solution(mesh):
    return jax.shard_map(
        on_device,
        mesh=mesh,
        in_specs=(
            P("fsdp", "ctx", None),
            P(),
            P("fsdp", None, None),
            P("fsdp", None, None),
            P(),
            P(),
            P(),
            P("fsdp", None),
            P("fsdp", "ctx", None),
        ),
        out_specs=(P("fsdp", "ctx", None), P(("fsdp", "ctx"), None), P(), P()),
        check_vma=False,
    )
```
